512 devices in a mesh: dp: 4 (over y), dev: 128 (over x, z, core).
Axes of the slice: x: 4, y: 4, z: 16, core: 2. Of those that a mesh axis runs over, the one named last changes fastest.
Arguments:
- frames: bfloat16 [512, 48, 8192], P(('dp', 'dev')), parts along dimension 0, may hold values from -6 to 6
- clip_ids: int32 [512], P(('dp', 'dev')), parts along dimension 0, may hold values from 0 to 11, never falling along the last dimension, each value on 1 to 17 neighbouring positions
- norm_gain: float32 [2, 64], replicated, may hold values from 0.25 to 1.75
- space_kernel: bfloat16 [2, 3, 3, 64, 64], replicated, may hold values from -0.25 to 0.25
- time_kernel: bfloat16 [2, 5, 64, 64], replicated, may hold values from -0.3125 to 0.3125
Outputs:
- encoded: bfloat16 [512, 48, 8192], P(('dp', 'dev')), parts along dimension 0
The draws below stay inside these ranges and needn't reach their ends.
There are 4 independent parts, one for each index of `dp`. The reference program is written for one: setup_inputs(seed, part) draws one part's arguments, and reference() takes and returns one part's arrays. A program takes and returns all parts, laid end to end along the dimension named above; an argument that names none is the same for every part. Nothing has to cross between parts.
Inputs may be any that keep to these rules, and one draw needn't show every extreme that they name: `clip_ids`: clip ids never fall along the frames; each clip holds 1 to 17 frames, one exactly 17.
All inputs are finite; a program needn't handle non-finite values.
Results may differ from the reference program's by a relative error of at most 0.0061.
Values may be sent and summed in bfloat16 or wider, within the bound.
A program may use at most 64 MiB of HBM per device.

```python
import math
import jax
import jax.numpy as jnp
import numpy as np
from jax import lax

C = 64
GROUPS = 32
W = 128
H = 48
TIME_TAPS = 5
TIME_DILATION = 2
BLOCKS = 2
FRAMES = 128
CLIPS = 12
CLIP_MOST = 17


def block_scale(rng, extent, pieces, least, top_value):
    loudness, own = 1.0, jax.random.fold_in(rng, 6)
    for dim, blocks in pieces:
        draws = jnp.exp(jax.random.uniform(jax.random.fold_in(own, dim), (blocks,), jnp.float32, least / len(pieces), top_value / len(pieces)))
        loudness = loudness * jnp.repeat(draws, extent[dim] // blocks).reshape([-1 if axis == dim else 1 for axis in range(len(extent))])
    return loudness


def split_up(number_of, total, reach, lean):
    portions = [(1 << 20) // math.isqrt(rank ** lean) + 1 for rank in range(2, number_of + 1)]
    spare, given = total - reach - (number_of - 1), [1] * (number_of - 1)
    while spare > 0:
        movable = [i for i in range(number_of - 1) if given[i] < reach]
        pool, left = sum([portions[i] for i in movable]), spare
        for i in movable:
            more = min(reach - given[i], max(1, left * portions[i] // pool), spare)
            given[i] = given[i] + more
            spare = spare - more
    return np.array([reach] + given)


def ragged_sizes(stream_key, amount, total, bound, slope):
    if amount == 2:
        one = jax.random.randint(stream_key, (), max(1, total - bound), min(bound, total - 1) + 1)
        return jnp.stack([one, total - one])
    lengths = jnp.asarray(split_up(amount, total, bound, slope), jnp.int32)
    couples = (amount - 1) // 2
    source_of, taker = lengths[1:1 + 2 * couples:2], lengths[2:2 + 2 * couples:2]
    margin = jnp.minimum(source_of - 1, bound - taker)
    passed = jax.random.randint(jax.random.fold_in(stream_key, 1), (couples,), 0, 1 << 20) % (margin + 1)
    lengths = lengths.at[1:1 + 2 * couples:2].set(source_of - passed).at[2:2 + 2 * couples:2].set(taker + passed)
    return lengths[jax.random.permutation(jax.random.fold_in(stream_key, 2), amount)]


def gaussian(key, dims, deviation, limit, shards=(), held_as=jnp.bfloat16):
    entries = jax.random.normal(key, dims, jnp.float32) * deviation
    if len(shards) > 0:
        entries = block_scale(key, dims, shards, -0.22, 0.18) * entries
    return jnp.clip(entries, min=-limit, max=limit).astype(held_as)


def setup_inputs(seed: int = 0, part: int = 0) -> dict:
    splits = jax.random.split(jax.random.key(seed), 6)
    part_splits = jax.random.split(jax.random.fold_in(splits[5], part), 6)
    frames = gaussian(part_splits[0], (FRAMES, H, W * C), 1.0, 6.0, ((0, 128),))
    clip_ids = jnp.searchsorted(jnp.cumsum(ragged_sizes(part_splits[1], CLIPS, FRAMES, CLIP_MOST, 2)), jnp.arange(FRAMES), side="right").astype(jnp.int32)
    norm_gain = jnp.clip(1.0 + 0.15 * jax.random.normal(splits[2], (BLOCKS, C), jnp.float32), 0.25, 1.75)
    space_kernel = gaussian(splits[3], (BLOCKS, 3, 3, C, C), (9 * C) ** -0.5, 0.25)
    time_kernel = gaussian(splits[4], (BLOCKS, TIME_TAPS, C, C), (TIME_TAPS * C) ** -0.5, 0.3125)
    return {"frames": frames, "clip_ids": clip_ids, "norm_gain": norm_gain, "space_kernel": space_kernel, "time_kernel": time_kernel}


def one_block(values, clip_ids, gain, space_w, time_w):
    frame_count = values.shape[0]
    xf = values.astype(jnp.float32).reshape(frame_count, H, W, C)
    grouped = xf.reshape(frame_count, H, W, GROUPS, C // GROUPS)
    center = lax.optimization_barrier(jnp.mean(grouped, axis=(1, 2, 4), keepdims=True))
    spread = lax.optimization_barrier(jnp.mean((grouped - center) * (grouped - center), axis=(1, 2, 4), keepdims=True))
    normal = ((grouped - center) / jnp.sqrt(spread + 1e-06)).reshape(frame_count, H, W, C)
    act = jax.nn.silu(normal * gain).astype(jnp.bfloat16)
    padded = jnp.pad(act, ((0, 0), (1, 1), (1, 1), (0, 0)))
    total = jnp.zeros((frame_count * H * W, C), jnp.float32)
    for i in range(3):
        for j in range(3):
            window = padded[:, i:i + H, j:j + W, :].reshape(-1, C)
            total = total + jnp.dot(window, space_w[i, j], preferred_element_type=jnp.float32)
    spat = total.astype(jnp.bfloat16).reshape(frame_count, H, W, C)
    index = jnp.arange(frame_count, dtype=jnp.int32)
    result = jnp.zeros((frame_count * H * W, C), jnp.float32)
    for kernel_step in range(TIME_TAPS):
        frame_offset = (kernel_step - TIME_TAPS // 2) * TIME_DILATION
        source = index + frame_offset
        inside = (source >= 0) & (source < frame_count)
        source = jnp.clip(source, 0, frame_count - 1).astype(jnp.int32)
        same = inside & (clip_ids[source] == clip_ids)
        moved = jnp.take(spat, source, axis=0) * same.astype(jnp.bfloat16)[:, None, None, None]
        result = result + jnp.dot(moved.reshape(-1, C), time_w[kernel_step], preferred_element_type=jnp.float32)
    update = lax.optimization_barrier(result.astype(jnp.bfloat16))
    summed = values.astype(jnp.float32) + update.astype(jnp.float32).reshape(values.shape)
    return summed.astype(jnp.bfloat16)

def reference(frames, clip_ids, norm_gain, space_kernel, time_kernel):
    current = frames
    for block_index in range(BLOCKS):
        current = one_block(current, clip_ids, norm_gain[block_index], space_kernel[block_index], time_kernel[block_index])
    return current
```

```python
import jax
import jax.numpy as jnp
from jax import lax
from jax.experimental import pallas as pl
from jax.experimental.pallas import tpu as pltpu
from jax.sharding import PartitionSpec as P

BLOCKS = 2
TAPS = 5
STEP = 2
GROUP = 2
PIECES = 8
EPS = 1e-06
MESH = pl.DeviceIdType.MESH
F32 = jnp.float32
BF16 = jnp.bfloat16
OFFSETS = (STEP, -STEP, 2 * STEP, -2 * STEP)
SLOT_OF_TAP = (2, 0, None, 1, 3)


def kernel(
    frames, clip, gain, space, time, out,
    x_buf, shifted, act, spat, came, bands, taps, my_id, ids, out_buf,
    send_sem, recv_sem, id_send, id_recv, out_sem,
):
    count = lax.axis_size("dev")
    me = lax.axis_index("dev")
    tiles, rows, lanes = x_buf.shape
    half = lanes // 2
    span = tiles // PIECES
    table_entries = rows * tiles * 2 * GROUP

    def peer(offset):
        return {"dev": lax.rem(me + offset + count, count)}

    barrier = pltpu.get_barrier_semaphore()
    for offset in OFFSETS:
        pl.semaphore_signal(barrier, inc=1, device_id=peer(offset), device_id_type=MESH)

    lane = lax.broadcasted_iota(jnp.int32, (1, lanes), 1)

    def whole_group(sums):
        both = sums + pltpu.roll(sums, half, 1)
        beside = jnp.where(lane % 2 == 0, pltpu.roll(both, lanes - 1, 1), pltpu.roll(both, 1, 1))
        return both + beside

    def piece(p):
        return pl.ds(pl.multiple_of(p * span, span), span)

    def take(p, sums):
        for t in range(span):
            at = pl.multiple_of((p * span + t) * lanes, lanes)
            tile = frames[0, :, pl.ds(at, lanes)]
            x_buf[p * span + t] = tile
            sums = sums + jnp.sum(tile.astype(F32), axis=0, keepdims=True)
        return sums

    sums = lax.fori_loop(0, PIECES, take, jnp.zeros((1, lanes), F32))

    my_id[...] = jnp.full(my_id.shape, clip[0], jnp.int32)
    shifted[...] = jnp.zeros_like(shifted)
    for r in range(3):
        act[r, 0] = jnp.zeros((rows, lanes), BF16)
        act[r, tiles + 1] = jnp.zeros((rows, lanes), BF16)
    bands[...] = jnp.zeros_like(bands)
    taps[...] = jnp.zeros_like(taps)

    def fill_bands(b):
        for r in range(3):
            for d in range(3):
                for a in range(2):
                    for c in range(2):
                        q = 2 * (d - 1) + a - c + 1
                        if 0 <= q <= 2:
                            at = (r * 3 + d) * lanes + a * half
                            bands[b, at : at + half, c * half : (c + 1) * half] = space[b, r, q]

    fill_bands(0)

    def id_copy(slot):
        return pltpu.make_async_remote_copy(
            src_ref=my_id, dst_ref=ids.at[slot], send_sem=id_send.at[slot], recv_sem=id_recv.at[slot],
            device_id=peer(OFFSETS[slot]), device_id_type=MESH,
        )

    def copy(b, slot, p):
        source = spat.at[b] if slot < 2 else came.at[b, slot - 2]
        return pltpu.make_async_remote_copy(
            src_ref=source.at[piece(p)], dst_ref=came.at[b, slot, piece(p)],
            send_sem=send_sem.at[b, slot, p], recv_sem=recv_sem.at[b, slot, p],
            device_id=peer(OFFSETS[slot % 2]), device_id_type=MESH,
        )

    def write_out(p):
        wide = span * lanes
        return pltpu.make_async_copy(
            out_buf.at[p], out.at[0, :, pl.ds(pl.multiple_of(p * wide, wide), wide)], out_sem.at[p]
        )

    for b in range(BLOCKS):
        mean = whole_group(sums) / table_entries

        def squares(p, total):
            off = x_buf[piece(p)].astype(F32) - mean
            return total + jnp.sum(off * off, axis=(0, 1))[None]

        spread = whole_group(lax.fori_loop(0, PIECES, squares, jnp.zeros((1, lanes), F32))) / table_entries
        gains = gain[b][None]
        scale = lax.rsqrt(spread + EPS) * jnp.concatenate([gains, gains], 1) * 0.5

        def activate(p):
            u = (x_buf[piece(p)].astype(F32) - mean) * scale
            value = u * (1.0 + jnp.tanh(u))
            shifted[:, 8 : 8 + rows] = value
            at = pl.ds(p * span + 1, span)
            act[1, at] = value.astype(BF16)
            act[0, at] = shifted[:, 7 : 7 + rows].astype(BF16)
            act[2, at] = shifted[:, 9 : 9 + rows].astype(BF16)

        def convolve(p):
            window = jnp.concatenate(
                [act[r, pl.ds(p * span + d, span)].reshape(span * rows, lanes) for r in range(3) for d in range(3)], 1
            )
            total = jnp.dot(window, bands[b], preferred_element_type=F32)
            spat[b, piece(p)] = total.astype(BF16).reshape(span, rows, lanes)

        activate(0)

        def make(p, carry):
            @pl.when(p + 1 < PIECES)
            def _():
                activate(p + 1)

            convolve(p)
            if b == 0:

                @pl.when(p == 0)
                def _():
                    pl.semaphore_wait(barrier, len(OFFSETS))

            copy(b, 0, p).start()
            copy(b, 1, p).start()
            return carry

        lax.fori_loop(0, PIECES, make, 0)

        if b == 0:
            for slot in range(4):
                id_copy(slot).start()
            for later in range(1, BLOCKS):
                fill_bands(later)
            for slot in range(4):
                id_copy(slot).wait()
            for k in range(TAPS):
                slot = SLOT_OF_TAP[k]
                for c in range(BLOCKS):
                    if slot is None:
                        matrix = time[c, k]
                    else:
                        other = me + (k - TAPS // 2) * STEP
                        inside = jnp.logical_and(other >= 0, other < count).astype(jnp.int32)
                        same = (ids[slot] == my_id[...]).astype(jnp.int32) * inside
                        keep = same[:1, :half].astype(F32)
                        matrix = (time[c, k].astype(F32) * keep).astype(BF16)
                    for a in range(2):
                        at = k * lanes + a * half
                        taps[c, at : at + half, a * half : (a + 1) * half] = matrix

        def forward(p, carry):
            for slot in range(2):
                copy(b, slot, p).wait_recv()
                copy(b, slot + 2, p).start()
            return carry

        lax.fori_loop(0, PIECES, forward, 0)

        def finish(p, sums):
            copy(b, 2, p).wait_recv()
            copy(b, 3, p).wait_recv()
            window = jnp.concatenate(
                [
                    (spat[b, piece(p)] if slot is None else came[b, slot, piece(p)]).reshape(span * rows, lanes)
                    for slot in SLOT_OF_TAP
                ],
                1,
            )
            update = jnp.dot(window, taps[b], preferred_element_type=F32).astype(BF16).astype(F32)
            value = (x_buf[piece(p)].astype(F32) + update.reshape(span, rows, lanes)).astype(BF16)
            if b + 1 < BLOCKS:
                x_buf[piece(p)] = value
                return sums + jnp.sum(value.astype(F32), axis=(0, 1))[None]
            for t in range(span):
                out_buf[p, :, t * lanes : (t + 1) * lanes] = value[t]
            write_out(p).start()
            return sums

        sums = lax.fori_loop(0, PIECES, finish, jnp.zeros((1, lanes), F32))

    def drain(p, carry):
        for b in range(BLOCKS):
            for slot in range(4):
                copy(b, slot, p).wait_send()
        write_out(p).wait()
        return carry

    lax.fori_loop(0, PIECES, drain, 0)


def per_device(frames, clip_ids, norm_gain, space_kernel, time_kernel):
    _, rows, wide = frames.shape
    lanes = 2 * space_kernel.shape[-1]
    tiles = wide // lanes
    span = tiles // PIECES
    vmem = pl.BlockSpec(memory_space=pltpu.VMEM)
    return pl.pallas_call(
        kernel,
        out_shape=jax.ShapeDtypeStruct(frames.shape, BF16),
        in_specs=[vmem, pl.BlockSpec(memory_space=pltpu.SMEM), vmem, vmem, vmem],
        out_specs=pl.BlockSpec(memory_space=pl.ANY),
        scratch_shapes=[
            pltpu.VMEM((tiles, rows, lanes), BF16),
            pltpu.VMEM((span, rows + 16, lanes), F32),
            pltpu.VMEM((3, tiles + 2, rows, lanes), BF16),
            pltpu.VMEM((BLOCKS, tiles, rows, lanes), BF16),
            pltpu.VMEM((BLOCKS, 4, tiles, rows, lanes), BF16),
            pltpu.VMEM((BLOCKS, 9 * lanes, lanes), BF16),
            pltpu.VMEM((BLOCKS, TAPS * lanes, lanes), BF16),
            pltpu.VMEM((8, lanes), jnp.int32),
            pltpu.VMEM((4, 8, lanes), jnp.int32),
            pltpu.VMEM((PIECES, rows, span * lanes), BF16),
            pltpu.SemaphoreType.DMA((BLOCKS, 4, PIECES)),
            pltpu.SemaphoreType.DMA((BLOCKS, 4, PIECES)),
            pltpu.SemaphoreType.DMA((4,)),
            pltpu.SemaphoreType.DMA((4,)),
            pltpu.SemaphoreType.DMA((PIECES,)),
        ],
        compiler_params=pltpu.CompilerParams(
            collective_id=0, has_side_effects=True, vmem_limit_bytes=40 << 20
        ),
        cost_estimate=pl.CostEstimate(flops=4_000_000_000, bytes_accessed=2_000_000, transcendentals=800_000),
    )(frames, clip_ids, norm_gain, space_kernel, time_kernel)


def solution(mesh):
    return jax.shard_map(
        per_device,
        mesh=mesh,
        in_specs=(P(("dp", "dev"), None, None), P(("dp", "dev")), P(), P(), P()),
        out_specs=P(("dp", "dev"), None, None),
        check_vma=False,
    )
```

```python
import jax
import jax.numpy as jnp
from jax import lax
from jax.experimental import pallas as pl
from jax.experimental.pallas import tpu as pltpu
from jax.sharding import PartitionSpec as P

BLOCKS = 2
TAPS = 5
STEP = 2
GROUP = 2
PIECES = 16
EARLY = 3
RAW_AT = 6
EPS = 1e-06
MESH = pl.DeviceIdType.MESH
F32 = jnp.float32
BF16 = jnp.bfloat16
OFFSETS = (STEP, -STEP, 2 * STEP, -2 * STEP)
SLOT_OF_TAP = (2, 0, None, 1, 3)


def kernel(
    frames_hbm, clip, gain_hbm, space_hbm, time_hbm, out,
    frames, gain, space, time,
    x_buf, shifted, act, spat, came, raw, bands, taps, facts, facts_in,
    load_sem, frame_sem, send_sem, recv_sem, raw_send, raw_recv, fact_send, fact_recv,
):
    count = lax.axis_size("dev")
    me = lax.axis_index("dev")
    tiles, rows, lanes = x_buf.shape
    half = lanes // 2
    span = tiles // PIECES
    wide = span * lanes
    early = raw.shape[2]
    table_entries = rows * tiles * 2 * GROUP

    def peer(offset):
        return {"dev": lax.rem(me + offset + count, count)}

    def here(offset):
        return jnp.logical_and(me + offset >= 0, me + offset < count)

    takes = [here(-offset) for offset in OFFSETS]
    gives = [here(STEP), here(-STEP)]
    gives += [jnp.logical_and(gives[0], takes[0]), jnp.logical_and(gives[1], takes[1])]

    def if_so(condition, action):
        pl.when(condition)(action)

    barrier = pltpu.get_barrier_semaphore()
    for offset in OFFSETS:

        @pl.when(here(offset))
        def _():
            pl.semaphore_signal(barrier, inc=1, device_id=peer(offset), device_id_type=MESH)

    def piece(p):
        return pl.ds(pl.multiple_of(p * span, span), span)

    def fetch(p):
        at = pl.ds(pl.multiple_of(p * wide, wide), wide)
        return pltpu.make_async_copy(frames_hbm.at[0, :, at], frames.at[:, at], frame_sem.at[p])

    def start_fetch(p, carry):
        fetch(p).start()
        return carry

    lax.fori_loop(0, PIECES, start_fetch, 0)
    loads = [
        pltpu.make_async_copy(source, target, load_sem.at[i])
        for i, (source, target) in enumerate(
            ((space_hbm, space), (gain_hbm, gain), (time_hbm, time))
        )
    ]
    for load in loads:
        load.start()

    def copy(b, slot, p):
        source = spat.at[b] if slot < 2 else came.at[b, slot - 2]
        return pltpu.make_async_remote_copy(
            src_ref=source.at[piece(p)], dst_ref=came.at[b, slot, piece(p)],
            send_sem=send_sem.at[b, slot, p], recv_sem=recv_sem.at[b, slot, p],
            device_id=peer(OFFSETS[slot % 2]), device_id_type=MESH,
        )

    def raw_copy(b, slot):
        source = x_buf.at[pl.ds(0, early)] if slot < 2 else raw.at[b, slot - 2]
        return pltpu.make_async_remote_copy(
            src_ref=source, dst_ref=raw.at[b, slot],
            send_sem=raw_send.at[b, slot], recv_sem=raw_recv.at[b, slot],
            device_id=peer(OFFSETS[slot % 2]), device_id_type=MESH,
        )

    def fact_copy(b, slot):
        return pltpu.make_async_remote_copy(
            src_ref=facts.at[b], dst_ref=facts_in.at[b, slot],
            send_sem=fact_send.at[b, slot], recv_sem=fact_recv.at[b, slot],
            device_id=peer(OFFSETS[slot]), device_id_type=MESH,
        )

    lane = lax.broadcasted_iota(jnp.int32, (1, lanes), 1)

    def whole_group(sums):
        both = sums + pltpu.roll(sums, half, 1)
        beside = jnp.where(lane % 2 == 0, pltpu.roll(both, lanes - 1, 1), pltpu.roll(both, 1, 1))
        return both + beside

    def take(p, sums):
        fetch(p).wait()
        for t in range(span):
            at = pl.multiple_of((p * span + t) * lanes, lanes)
            tile = frames[:, pl.ds(at, lanes)]
            x_buf[p * span + t] = tile
            sums = sums + jnp.sum(tile.astype(F32), axis=0, keepdims=True)
        return sums

    sums = lax.fori_loop(0, EARLY + 1, take, jnp.zeros((1, lanes), F32))
    pl.semaphore_wait(barrier, sum(here(offset).astype(jnp.int32) for offset in OFFSETS))
    for slot in range(2):
        if_so(gives[slot], raw_copy(0, slot).start)
    sums = lax.fori_loop(EARLY + 1, PIECES, take, sums)

    shifted[...] = jnp.zeros_like(shifted)
    for r in range(3):
        act[r, 0] = jnp.zeros((rows, lanes), BF16)
        act[r, tiles + 1] = jnp.zeros((rows, lanes), BF16)
    bands[...] = jnp.zeros_like(bands)

    def fill_bands(b):
        for r in range(3):
            for d in range(3):
                for a in range(2):
                    for c in range(2):
                        q = 2 * (d - 1) + a - c + 1
                        if 0 <= q <= 2:
                            at = (r * 3 + d) * lanes + a * half
                            bands[b, at : at + half, c * half : (c + 1) * half] = space[b, r, q]

    def activate(values, at, mean, scale):
        n = values.shape[0]
        u = (values.astype(F32) - mean) * scale
        value = u * (1.0 + jnp.tanh(u))
        shifted[:n, 8 : 8 + rows] = value
        where = pl.ds(at + 1, n)
        act[1, where] = value.astype(BF16)
        act[0, where] = shifted[:n, 7 : 7 + rows].astype(BF16)
        act[2, where] = shifted[:n, 9 : 9 + rows].astype(BF16)

    def convolve(b, p):
        window = jnp.concatenate(
            [act[r, pl.ds(p * span + d, span)].reshape(span * rows, lanes) for r in range(3) for d in range(3)], 1
        )
        total = jnp.dot(window, bands[b], preferred_element_type=F32)
        return total.astype(BF16).reshape(span, rows, lanes)

    loads[0].wait()
    fill_bands(0)
    loads[1].wait()

    for b in range(BLOCKS):
        mean = whole_group(sums) / table_entries

        def squares(p, total):
            off = x_buf[piece(p)].astype(F32) - mean
            return total + jnp.sum(off * off, axis=(0, 1))[None]

        spread = whole_group(lax.fori_loop(0, PIECES, squares, jnp.zeros((1, lanes), F32))) / table_entries
        gains = gain[b : b + 1]
        scale = lax.rsqrt(spread + EPS) * jnp.concatenate([gains, gains], 1) * 0.5
        facts[b, 0:1] = mean
        facts[b, 1:2] = scale
        facts[b, 2:8] = jnp.full((6, lanes), clip[0], jnp.int32).astype(F32)
        for slot in range(4):
            if_so(here(OFFSETS[slot]), fact_copy(b, slot).start)

        def own(p):
            activate(x_buf[piece(p)], p * span, mean, scale)

        own(EARLY - 1)
        own(EARLY)

        def make(p, carry):
            @pl.when(p + 1 < PIECES)
            def _():
                own(p + 1)

            spat[b, piece(p)] = convolve(b, p)
            for slot in range(2):
                if_so(gives[slot], copy(b, slot, p).start)
            return carry

        lax.fori_loop(EARLY, PIECES, make, 0)

        for slot in range(2):
            if_so(takes[slot], raw_copy(b, slot).wait_recv)
            if_so(gives[slot + 2], raw_copy(b, slot + 2).start)

        def own_early(p, carry):
            own(p)
            return carry

        lax.fori_loop(0, EARLY - 1, own_early, 0)

        def make_early(p, carry):
            spat[b, piece(p)] = convolve(b, p)
            return carry

        lax.fori_loop(0, EARLY, make_early, 0)

        def redo(slot):
            if slot > 1:
                raw_copy(b, slot).wait_recv()
            fact_copy(b, slot).wait_recv()
            mean = facts_in[b, slot, 0:1]
            scale = facts_in[b, slot, 1:2]

            def norm(p, carry):
                activate(raw[b, slot, piece(p)], p * span, mean, scale)
                return carry

            lax.fori_loop(0, EARLY, norm, 0)
            activate(raw[b, slot, EARLY * span :], EARLY * span, mean, scale)

            def conv(p, carry):
                came[b, slot, piece(p)] = convolve(b, p)
                return carry

            lax.fori_loop(0, EARLY, conv, 0)

        def redo_or_blank(slot):
            if_so(takes[slot], lambda: redo(slot))

            @pl.when(jnp.logical_not(takes[slot]))
            def _():
                came[b, slot] = jnp.zeros((tiles, rows, lanes), BF16)

        redo_or_blank(0)
        redo_or_blank(1)

        def forward(p, carry):
            for slot in range(2):
                if_so(takes[slot], copy(b, slot, p).wait_recv)
                if_so(gives[slot + 2], copy(b, slot + 2, p).start)
            return carry

        lax.fori_loop(EARLY, PIECES, forward, 0)

        redo_or_blank(2)
        redo_or_blank(3)

        if b == 0:
            for slot in range(2):
                if_so(gives[slot], raw_copy(b, slot).wait_send)
            for later in range(1, BLOCKS):
                fill_bands(later)
            loads[2].wait()
            taps[...] = jnp.zeros_like(taps)
            for k in range(TAPS):
                slot = SLOT_OF_TAP[k]
                for c in range(BLOCKS):
                    if slot is None:
                        matrix = time[c, k]
                    else:
                        inside = here((k - TAPS // 2) * STEP).astype(F32)
                        same = (facts_in[0, slot, 2:3, :half] == facts[0, 2:3, :half]).astype(F32)
                        matrix = (time[c, k].astype(F32) * (same * inside)).astype(BF16)
                    for a in range(2):
                        at = k * lanes + a * half
                        taps[c, at : at + half, a * half : (a + 1) * half] = matrix

        def finish(p, sums):
            window = jnp.concatenate(
                [
                    (spat[b, piece(p)] if slot is None else came[b, slot, piece(p)]).reshape(span * rows, lanes)
                    for slot in SLOT_OF_TAP
                ],
                1,
            )
            update = jnp.dot(window, taps[b], preferred_element_type=F32).astype(BF16).astype(F32)
            value = (x_buf[piece(p)].astype(F32) + update.reshape(span, rows, lanes)).astype(BF16)
            if b + 1 < BLOCKS:
                x_buf[piece(p)] = value
                return sums + jnp.sum(value.astype(F32), axis=(0, 1))[None]
            for t in range(span):
                at = pl.multiple_of((p * span + t) * lanes, lanes)
                out[0, :, pl.ds(at, lanes)] = value[t]
            return sums

        def finish_arrived(p, sums):
            if b + 1 < BLOCKS:

                for slot in range(2):
                    if_so(jnp.logical_and(p == RAW_AT, gives[slot]), raw_copy(b + 1, slot).start)

            for slot in (2, 3):
                if_so(takes[slot], copy(b, slot, p).wait_recv)
            return finish(p, sums)

        sums = lax.fori_loop(0, EARLY, finish, jnp.zeros((1, lanes), F32))
        sums = lax.fori_loop(EARLY, PIECES, finish_arrived, sums)

    for b in range(BLOCKS):
        for slot in range(4):
            if_so(here(OFFSETS[slot]), fact_copy(b, slot).wait_send)
            if b > 0 or slot > 1:
                if_so(gives[slot], raw_copy(b, slot).wait_send)

    def drain(p, carry):
        for b in range(BLOCKS):
            for slot in range(4):
                if_so(gives[slot], copy(b, slot, p).wait_send)
        return carry

    lax.fori_loop(EARLY, PIECES, drain, 0)


def per_device(frames, clip_ids, norm_gain, space_kernel, time_kernel):
    _, rows, wide = frames.shape
    lanes = 2 * space_kernel.shape[-1]
    tiles = wide // lanes
    span = tiles // PIECES
    early = EARLY * span + 1
    hbm = pl.BlockSpec(memory_space=pl.ANY)
    frames, norm_gain, space_kernel, time_kernel = (
        pltpu.with_memory_space_constraint(x, pltpu.HBM) for x in (frames, norm_gain, space_kernel, time_kernel)
    )
    return pl.pallas_call(
        kernel,
        out_shape=jax.ShapeDtypeStruct(frames.shape, BF16),
        in_specs=[hbm, pl.BlockSpec(memory_space=pltpu.SMEM), hbm, hbm, hbm],
        out_specs=pl.BlockSpec(memory_space=pltpu.VMEM),
        scratch_shapes=[
            pltpu.VMEM((rows, wide), BF16),
            pltpu.VMEM(norm_gain.shape, F32),
            pltpu.VMEM(space_kernel.shape, BF16),
            pltpu.VMEM(time_kernel.shape, BF16),
            pltpu.VMEM((tiles, rows, lanes), BF16),
            pltpu.VMEM((span, rows + 16, lanes), F32),
            pltpu.VMEM((3, tiles + 2, rows, lanes), BF16),
            pltpu.VMEM((BLOCKS, tiles, rows, lanes), BF16),
            pltpu.VMEM((BLOCKS, 4, tiles, rows, lanes), BF16),
            pltpu.VMEM((BLOCKS, 4, early, rows, lanes), BF16),
            pltpu.VMEM((BLOCKS, 9 * lanes, lanes), BF16),
            pltpu.VMEM((BLOCKS, TAPS * lanes, lanes), BF16),
            pltpu.VMEM((BLOCKS, 8, lanes), F32),
            pltpu.VMEM((BLOCKS, 4, 8, lanes), F32),
            pltpu.SemaphoreType.DMA((3,)),
            pltpu.SemaphoreType.DMA((PIECES,)),
            pltpu.SemaphoreType.DMA((BLOCKS, 4, PIECES)),
            pltpu.SemaphoreType.DMA((BLOCKS, 4, PIECES)),
            pltpu.SemaphoreType.DMA((BLOCKS, 4)),
            pltpu.SemaphoreType.DMA((BLOCKS, 4)),
            pltpu.SemaphoreType.DMA((BLOCKS, 4)),
            pltpu.SemaphoreType.DMA((BLOCKS, 4)),
        ],
        compiler_params=pltpu.CompilerParams(
            collective_id=0, has_side_effects=True, vmem_limit_bytes=48 << 20
        ),
        cost_estimate=pl.CostEstimate(flops=5_000_000_000, bytes_accessed=2_000_000, transcendentals=800_000),
    )(frames, clip_ids, norm_gain, space_kernel, time_kernel)


def solution(mesh):
    return jax.shard_map(
        per_device,
        mesh=mesh,
        in_specs=(P(("dp", "dev"), None, None), P(("dp", "dev")), P(), P(), P()),
        out_specs=P(("dp", "dev"), None, None),
        check_vma=False,
    )
```

```python
import jax
import jax.numpy as jnp
from jax import lax
from jax.experimental import pallas as pl
from jax.experimental.pallas import tpu as pltpu
from jax.sharding import PartitionSpec as P

BLOCKS = 2
TAPS = 5
STEP = 2
GROUP = 2
PIECES = 16
EARLY = 4
RAW_AT = 8
RUNS = (((4, 8), (8, 12), (12, 16)), ((4, 8), (8, 12), (12, 15), (15, 16)))
EPS = 1e-06
MESH = pl.DeviceIdType.MESH
F32 = jnp.float32
BF16 = jnp.bfloat16
OFFSETS = (STEP, -STEP, 2 * STEP, -2 * STEP)
SLOT_OF_TAP = (2, 0, None, 1, 3)


def kernel(
    frames_hbm, clip, gain_hbm, space_hbm, time_hbm, out,
    frames, gain, space, time,
    x_buf, shifted, act, spat, came, raw, bands, taps, facts, facts_in,
    load_sem, frame_sem, send_sem, recv_sem, raw_send, raw_recv, fact_send, fact_recv,
):
    count = lax.axis_size("dev")
    me = lax.axis_index("dev")
    tiles, rows, lanes = x_buf.shape
    half = lanes // 2
    span = tiles // PIECES
    wide = span * lanes
    early = raw.shape[2]
    table_entries = rows * tiles * 2 * GROUP

    def peer(offset):
        return {"dev": lax.rem(me + offset + count, count)}

    def here(offset):
        return jnp.logical_and(me + offset >= 0, me + offset < count)

    takes = [here(-offset) for offset in OFFSETS]
    gives = [here(STEP), here(-STEP)]
    gives += [jnp.logical_and(gives[0], takes[0]), jnp.logical_and(gives[1], takes[1])]

    def if_so(condition, action):
        pl.when(condition)(action)

    barrier = pltpu.get_barrier_semaphore()
    for offset in OFFSETS:

        @pl.when(here(offset))
        def _():
            pl.semaphore_signal(barrier, inc=1, device_id=peer(offset), device_id_type=MESH)

    def piece(p):
        return pl.ds(pl.multiple_of(p * span, span), span)

    def fetch(p):
        at = pl.ds(pl.multiple_of(p * wide, wide), wide)
        return pltpu.make_async_copy(frames_hbm.at[0, :, at], frames.at[:, at], frame_sem.at[p])

    def start_fetch(p, carry):
        fetch(p).start()
        return carry

    lax.fori_loop(0, PIECES, start_fetch, 0)
    loads = [
        pltpu.make_async_copy(source, target, load_sem.at[i])
        for i, (source, target) in enumerate(
            ((space_hbm, space), (gain_hbm, gain), (time_hbm, time))
        )
    ]
    for load in loads:
        load.start()

    shifted[...] = jnp.zeros_like(shifted)
    for r in range(3):
        act[r, 0] = jnp.zeros((rows, lanes), BF16)
        act[r, tiles + 1] = jnp.zeros((rows, lanes), BF16)
    bands[...] = jnp.zeros_like(bands)

    def copy(b, slot, run):
        first, last = RUNS[b][run]
        part = pl.ds(first * span, (last - first) * span)
        source = spat.at[b] if slot < 2 else came.at[b, slot - 2]
        return pltpu.make_async_remote_copy(
            src_ref=source.at[part], dst_ref=came.at[b, slot, part],
            send_sem=send_sem.at[b, slot, run], recv_sem=recv_sem.at[b, slot, run],
            device_id=peer(OFFSETS[slot % 2]), device_id_type=MESH,
        )

    def raw_copy(b, slot):
        source = x_buf.at[pl.ds(0, early)] if slot < 2 else raw.at[b, slot - 2]
        return pltpu.make_async_remote_copy(
            src_ref=source, dst_ref=raw.at[b, slot],
            send_sem=raw_send.at[b, slot], recv_sem=raw_recv.at[b, slot],
            device_id=peer(OFFSETS[slot % 2]), device_id_type=MESH,
        )

    def fact_copy(b, slot):
        return pltpu.make_async_remote_copy(
            src_ref=facts.at[b], dst_ref=facts_in.at[b, slot],
            send_sem=fact_send.at[b, slot], recv_sem=fact_recv.at[b, slot],
            device_id=peer(OFFSETS[slot]), device_id_type=MESH,
        )

    lane = lax.broadcasted_iota(jnp.int32, (1, lanes), 1)

    def whole_group(sums):
        sums = jnp.sum(sums, axis=0, keepdims=True)
        both = sums + pltpu.roll(sums, half, 1)
        beside = jnp.where(lane % 2 == 0, pltpu.roll(both, lanes - 1, 1), pltpu.roll(both, 1, 1))
        return both + beside

    def by_eight(values):
        return jnp.sum(values.reshape(-1, 8, lanes), axis=0)

    no_sums = jnp.zeros((8, lanes), F32)

    def take(p, sums):
        fetch(p).wait()
        for t in range(span):
            at = pl.multiple_of((p * span + t) * lanes, lanes)
            tile = frames[:, pl.ds(at, lanes)]
            x_buf[p * span + t] = tile
            sums = sums + by_eight(tile.astype(F32))
        return sums

    sums = lax.fori_loop(0, EARLY + 1, take, no_sums)
    pl.semaphore_wait(barrier, sum(here(offset).astype(jnp.int32) for offset in OFFSETS))
    for slot in range(2):
        if_so(gives[slot], raw_copy(0, slot).start)
    sums = lax.fori_loop(EARLY + 1, PIECES, take, sums)

    def fill_bands(b):
        for r in range(3):
            for d in range(3):
                for a in range(2):
                    for c in range(2):
                        q = 2 * (d - 1) + a - c + 1
                        if 0 <= q <= 2:
                            at = (r * 3 + d) * lanes + a * half
                            bands[b, at : at + half, c * half : (c + 1) * half] = space[b, r, q]

    def activate(values, at, mean, scale):
        n = values.shape[0]
        u = (values.astype(F32) - mean) * scale
        value = u * (1.0 + jnp.tanh(u))
        shifted[:n, 8 : 8 + rows] = value
        where = pl.ds(at + 1, n)
        act[1, where] = value.astype(BF16)
        act[0, where] = shifted[:n, 7 : 7 + rows].astype(BF16)
        act[2, where] = shifted[:n, 9 : 9 + rows].astype(BF16)

    def convolve(b, p):
        window = jnp.concatenate(
            [act[r, pl.ds(p * span + d, span)].reshape(span * rows, lanes) for r in range(3) for d in range(3)], 1
        )
        total = jnp.dot(window, bands[b], preferred_element_type=F32)
        return total.astype(BF16).reshape(span, rows, lanes)

    loads[0].wait()
    fill_bands(0)
    loads[1].wait()

    for b in range(BLOCKS):
        mean = whole_group(sums) / table_entries

        def squares(p, total):
            off = x_buf[piece(p)].astype(F32) - mean
            return total + by_eight(off * off)

        spread = whole_group(lax.fori_loop(0, PIECES, squares, no_sums)) / table_entries
        gains = gain[b : b + 1]
        scale = lax.rsqrt(spread + EPS) * jnp.concatenate([gains, gains], 1) * 0.5
        facts[b, 0:1] = mean
        facts[b, 1:2] = scale
        facts[b, 2:8] = jnp.full((6, lanes), clip[0], jnp.int32).astype(F32)
        for slot in range(4):
            if_so(here(OFFSETS[slot]), fact_copy(b, slot).start)

        def own(p):
            activate(x_buf[piece(p)], p * span, mean, scale)

        own(EARLY - 1)
        own(EARLY)

        def make(p, carry):
            @pl.when(p + 1 < PIECES)
            def _():
                own(p + 1)

            spat[b, piece(p)] = convolve(b, p)
            for run, (_, last) in enumerate(RUNS[b]):
                for slot in range(2):
                    if_so(jnp.logical_and(p == last - 1, gives[slot]), copy(b, slot, run).start)
            return carry

        lax.fori_loop(EARLY, PIECES, make, 0)

        for slot in range(2):
            if_so(takes[slot], raw_copy(b, slot).wait_recv)
            if_so(gives[slot + 2], raw_copy(b, slot + 2).start)

        def own_early(p, carry):
            own(p)
            return carry

        lax.fori_loop(0, EARLY - 1, own_early, 0)

        def make_early(p, carry):
            spat[b, piece(p)] = convolve(b, p)
            return carry

        lax.fori_loop(0, EARLY, make_early, 0)

        def redo(slot):
            if slot > 1:
                raw_copy(b, slot).wait_recv()
            fact_copy(b, slot).wait_recv()
            mean = facts_in[b, slot, 0:1]
            scale = facts_in[b, slot, 1:2]

            def norm(p, carry):
                activate(raw[b, slot, piece(p)], p * span, mean, scale)
                return carry

            lax.fori_loop(0, EARLY, norm, 0)
            activate(raw[b, slot, EARLY * span :], EARLY * span, mean, scale)

            def conv(p, carry):
                came[b, slot, piece(p)] = convolve(b, p)
                return carry

            lax.fori_loop(0, EARLY, conv, 0)

        def redo_or_blank(slot):
            if_so(takes[slot], lambda: redo(slot))

            @pl.when(jnp.logical_not(takes[slot]))
            def _():
                came[b, slot] = jnp.zeros((tiles, rows, lanes), BF16)

        redo_or_blank(0)
        redo_or_blank(1)

        for run in range(len(RUNS[b])):
            for slot in range(2):
                if_so(takes[slot], copy(b, slot, run).wait_recv)
                if_so(gives[slot + 2], copy(b, slot + 2, run).start)

        redo_or_blank(2)
        redo_or_blank(3)

        if b == 0:
            for slot in range(2):
                if_so(gives[slot], raw_copy(b, slot).wait_send)
            for later in range(1, BLOCKS):
                fill_bands(later)
            loads[2].wait()
            taps[...] = jnp.zeros_like(taps)
            for k in range(TAPS):
                slot = SLOT_OF_TAP[k]
                for c in range(BLOCKS):
                    if slot is None:
                        matrix = time[c, k]
                    else:
                        inside = here((k - TAPS // 2) * STEP).astype(F32)
                        same = (facts_in[0, slot, 2:3, :half] == facts[0, 2:3, :half]).astype(F32)
                        matrix = (time[c, k].astype(F32) * (same * inside)).astype(BF16)
                    for a in range(2):
                        at = k * lanes + a * half
                        taps[c, at : at + half, a * half : (a + 1) * half] = matrix

        def finish(p, sums):
            window = jnp.concatenate(
                [
                    (spat[b, piece(p)] if slot is None else came[b, slot, piece(p)]).reshape(span * rows, lanes)
                    for slot in SLOT_OF_TAP
                ],
                1,
            )
            update = jnp.dot(window, taps[b], preferred_element_type=F32).astype(BF16).astype(F32)
            value = (x_buf[piece(p)].astype(F32) + update.reshape(span, rows, lanes)).astype(BF16)
            if b + 1 < BLOCKS:
                x_buf[piece(p)] = value
                return sums + by_eight(value.astype(F32))
            for t in range(span):
                at = pl.multiple_of((p * span + t) * lanes, lanes)
                out[0, :, pl.ds(at, lanes)] = value[t]
            return sums

        def finish_arrived(p, sums):
            if b + 1 < BLOCKS:

                for slot in range(2):
                    if_so(jnp.logical_and(p == RAW_AT, gives[slot]), raw_copy(b + 1, slot).start)

            for run, (first, _) in enumerate(RUNS[b]):
                for slot in (2, 3):
                    if_so(jnp.logical_and(p == first, takes[slot]), copy(b, slot, run).wait_recv)
            return finish(p, sums)

        sums = lax.fori_loop(0, EARLY, finish, no_sums)
        sums = lax.fori_loop(EARLY, PIECES, finish_arrived, sums)

    for b in range(BLOCKS):
        for slot in range(4):
            if_so(here(OFFSETS[slot]), fact_copy(b, slot).wait_send)
            if b > 0 or slot > 1:
                if_so(gives[slot], raw_copy(b, slot).wait_send)

            for run in range(len(RUNS[b])):
                if_so(gives[slot], copy(b, slot, run).wait_send)


def per_device(frames, clip_ids, norm_gain, space_kernel, time_kernel):
    _, rows, wide = frames.shape
    lanes = 2 * space_kernel.shape[-1]
    tiles = wide // lanes
    span = tiles // PIECES
    early = EARLY * span + 1
    hbm = pl.BlockSpec(memory_space=pl.ANY)
    frames, norm_gain, space_kernel, time_kernel = (
        pltpu.with_memory_space_constraint(x, pltpu.HBM) for x in (frames, norm_gain, space_kernel, time_kernel)
    )
    return pl.pallas_call(
        kernel,
        out_shape=jax.ShapeDtypeStruct(frames.shape, BF16),
        in_specs=[hbm, pl.BlockSpec(memory_space=pltpu.SMEM), hbm, hbm, hbm],
        out_specs=pl.BlockSpec(memory_space=pltpu.VMEM),
        scratch_shapes=[
            pltpu.VMEM((rows, wide), BF16),
            pltpu.VMEM(norm_gain.shape, F32),
            pltpu.VMEM(space_kernel.shape, BF16),
            pltpu.VMEM(time_kernel.shape, BF16),
            pltpu.VMEM((tiles, rows, lanes), BF16),
            pltpu.VMEM((span, rows + 16, lanes), F32),
            pltpu.VMEM((3, tiles + 2, rows, lanes), BF16),
            pltpu.VMEM((BLOCKS, tiles, rows, lanes), BF16),
            pltpu.VMEM((BLOCKS, 4, tiles, rows, lanes), BF16),
            pltpu.VMEM((BLOCKS, 4, early, rows, lanes), BF16),
            pltpu.VMEM((BLOCKS, 9 * lanes, lanes), BF16),
            pltpu.VMEM((BLOCKS, TAPS * lanes, lanes), BF16),
            pltpu.VMEM((BLOCKS, 8, lanes), F32),
            pltpu.VMEM((BLOCKS, 4, 8, lanes), F32),
            pltpu.SemaphoreType.DMA((3,)),
            pltpu.SemaphoreType.DMA((PIECES,)),
            pltpu.SemaphoreType.DMA((BLOCKS, 4, 4)),
            pltpu.SemaphoreType.DMA((BLOCKS, 4, 4)),
            pltpu.SemaphoreType.DMA((BLOCKS, 4)),
            pltpu.SemaphoreType.DMA((BLOCKS, 4)),
            pltpu.SemaphoreType.DMA((BLOCKS, 4)),
            pltpu.SemaphoreType.DMA((BLOCKS, 4)),
        ],
        compiler_params=pltpu.CompilerParams(
            collective_id=0, has_side_effects=True, vmem_limit_bytes=48 << 20
        ),
        cost_estimate=pl.CostEstimate(flops=5_000_000_000, bytes_accessed=2_000_000, transcendentals=800_000),
    )(frames, clip_ids, norm_gain, space_kernel, time_kernel)


def solution(mesh):
    return jax.shard_map(
        per_device,
        mesh=mesh,
        in_specs=(P(("dp", "dev"), None, None), P(("dp", "dev")), P(), P(), P()),
        out_specs=P(("dp", "dev"), None, None),
        check_vma=False,
    )
```

```python
import jax
import jax.numpy as jnp
from jax import lax
from jax.experimental import pallas as pl
from jax.experimental.pallas import tpu as pltpu
from jax.sharding import PartitionSpec as P

BLOCKS = 2
TAPS = 5
STEP = 2
GROUP = 2
PIECES = 16
EARLY = 4
RAW_AT = 8
LINE = 32
RUNS = (((4, 8), (8, 12), (12, 16)), ((4, 8), (8, 12), (12, 15), (15, 16)))
EPS = 1e-06
MESH = pl.DeviceIdType.MESH
F32 = jnp.float32
BF16 = jnp.bfloat16
OFFSETS = (STEP, -STEP, 2 * STEP, -2 * STEP)
SLOT_OF_TAP = (2, 0, None, 1, 3)


def kernel(
    frames_hbm, clip, gain_hbm, space_hbm, time_hbm, out,
    frames, gain, space, time,
    x_buf, shifted, act, spat, came, raw, bands, taps, facts, facts_in, passing,
    load_sem, frame_sem, send_sem, recv_sem, raw_send, raw_recv, fact_send, fact_recv,
    pass_send, pass_recv, ready,
):
    count = lax.axis_size("dev")
    me = lax.axis_index("dev")
    tiles, rows, lanes = x_buf.shape
    half = lanes // 2
    span = tiles // PIECES
    wide = span * lanes
    early = raw.shape[2]
    table_entries = rows * tiles * 2 * GROUP

    def peer(offset):
        return {"dev": lax.rem(me + offset + count, count)}

    def here(offset):
        return jnp.logical_and(me + offset >= 0, me + offset < count)

    takes = [here(-offset) for offset in OFFSETS]
    gives = [here(STEP), here(-STEP)]
    gives += [jnp.logical_and(gives[0], takes[0]), jnp.logical_and(gives[1], takes[1])]

    def if_so(condition, action):
        pl.when(condition)(action)

    line = me // LINE
    at_start = lax.rem(me, LINE) < STEP
    at_end = lax.rem(me, LINE) >= LINE - STEP
    sends_aside = jnp.logical_and(at_end, me + LINE < count)
    passes_on = jnp.logical_and(at_end, me >= LINE)
    from_aside = jnp.logical_and(at_start, me >= LINE)

    def aside(run, source_line):
        return run >= 2 - source_line

    barrier = pltpu.get_barrier_semaphore()

    def arrive(offset):
        pl.semaphore_signal(barrier, inc=1, device_id=peer(offset), device_id_type=MESH)

    if_so(here(-STEP), lambda: arrive(-STEP))
    if_so(passes_on, lambda: arrive(-LINE))
    if_so(from_aside, lambda: arrive(LINE - STEP))

    def piece(p):
        return pl.ds(pl.multiple_of(p * span, span), span)

    def fetch(p):
        at = pl.ds(pl.multiple_of(p * wide, wide), wide)
        return pltpu.make_async_copy(frames_hbm.at[0, :, at], frames.at[:, at], frame_sem.at[p])

    def start_fetch(p, carry):
        fetch(p).start()
        return carry

    lax.fori_loop(0, PIECES, start_fetch, 0)
    loads = [
        pltpu.make_async_copy(source, target, load_sem.at[i])
        for i, (source, target) in enumerate(
            ((space_hbm, space), (gain_hbm, gain), (time_hbm, time))
        )
    ]
    for load in loads:
        load.start()

    shifted[...] = jnp.zeros_like(shifted)
    for r in range(3):
        act[r, 0] = jnp.zeros((rows, lanes), BF16)
        act[r, tiles + 1] = jnp.zeros((rows, lanes), BF16)
    bands[...] = jnp.zeros_like(bands)

    def copy(b, slot, run):
        first, last = RUNS[b][run]
        part = pl.ds(first * span, (last - first) * span)
        source = spat.at[b] if slot < 2 else came.at[b, slot - 2]
        return pltpu.make_async_remote_copy(
            src_ref=source.at[part], dst_ref=came.at[b, slot, part],
            send_sem=send_sem.at[b, slot, run], recv_sem=recv_sem.at[b, slot, run],
            device_id=peer(OFFSETS[slot % 2]), device_id_type=MESH,
        )

    def raw_copy(b, slot):
        source = x_buf.at[pl.ds(0, early)] if slot < 2 else raw.at[b, slot - 2]
        return pltpu.make_async_remote_copy(
            src_ref=source, dst_ref=raw.at[b, slot],
            send_sem=raw_send.at[b, slot], recv_sem=raw_recv.at[b, slot],
            device_id=peer(OFFSETS[slot % 2]), device_id_type=MESH,
        )

    def fact_copy(b, slot):
        source = facts.at[b] if slot < 2 else facts_in.at[b, slot - 2]
        return pltpu.make_async_remote_copy(
            src_ref=source, dst_ref=facts_in.at[b, slot],
            send_sem=fact_send.at[b, slot], recv_sem=fact_recv.at[b, slot],
            device_id=peer(OFFSETS[slot % 2]), device_id_type=MESH,
        )

    def copy_aside(b, run):
        first, last = RUNS[b][run]
        part = pl.ds(first * span, (last - first) * span)
        return pltpu.make_async_remote_copy(
            src_ref=spat.at[b, part], dst_ref=passing.at[b, part],
            send_sem=send_sem.at[b, 0, run], recv_sem=pass_recv.at[b, run],
            device_id=peer(LINE), device_id_type=MESH,
        )

    def pass_on(b, run):
        first, last = RUNS[b][run]
        part = pl.ds(first * span, (last - first) * span)
        return pltpu.make_async_remote_copy(
            src_ref=passing.at[b, part], dst_ref=came.at[b, 0, part],
            send_sem=pass_send.at[b, run], recv_sem=recv_sem.at[b, 0, run],
            device_id=peer(STEP - LINE), device_id_type=MESH,
        )

    lane = lax.broadcasted_iota(jnp.int32, (1, lanes), 1)

    def whole_group(sums):
        sums = jnp.sum(sums, axis=0, keepdims=True)
        both = sums + pltpu.roll(sums, half, 1)
        beside = jnp.where(lane % 2 == 0, pltpu.roll(both, lanes - 1, 1), pltpu.roll(both, 1, 1))
        return both + beside

    def by_eight(values):
        return jnp.sum(values.reshape(-1, 8, lanes), axis=0)

    no_sums = jnp.zeros((8, lanes), F32)

    def take(p, sums):
        fetch(p).wait()
        for t in range(span):
            at = pl.multiple_of((p * span + t) * lanes, lanes)
            tile = frames[:, pl.ds(at, lanes)]
            x_buf[p * span + t] = tile
            sums = sums + by_eight(tile.astype(F32))
        return sums

    sums = lax.fori_loop(0, EARLY + 1, take, no_sums)
    pl.semaphore_wait(barrier, sum(c.astype(jnp.int32) for c in (gives[0], sends_aside, passes_on)))

    @pl.when(gives[0])
    def _():
        pl.semaphore_signal(ready, inc=1, device_id=peer(STEP), device_id_type=MESH)
        raw_copy(0, 0).start()

    soon = jnp.logical_and(gives[1], jnp.logical_not(at_start))
    late = jnp.logical_and(gives[1], at_start)

    @pl.when(soon)
    def _():
        pl.semaphore_wait(ready, 1)
        raw_copy(0, 1).start()
    sums = lax.fori_loop(EARLY + 1, PIECES, take, sums)

    def fill_bands(b):
        for r in range(3):
            for d in range(3):
                for a in range(2):
                    for c in range(2):
                        q = 2 * (d - 1) + a - c + 1
                        if 0 <= q <= 2:
                            at = (r * 3 + d) * lanes + a * half
                            bands[b, at : at + half, c * half : (c + 1) * half] = space[b, r, q]

    def activate(values, at, mean, scale):
        n = values.shape[0]
        u = (values.astype(F32) - mean) * scale
        value = u * (1.0 + jnp.tanh(u))
        shifted[:n, 8 : 8 + rows] = value
        where = pl.ds(at + 1, n)
        act[1, where] = value.astype(BF16)
        act[0, where] = shifted[:n, 7 : 7 + rows].astype(BF16)
        act[2, where] = shifted[:n, 9 : 9 + rows].astype(BF16)

    def convolve(b, p):
        window = jnp.concatenate(
            [act[r, pl.ds(p * span + d, span)].reshape(span * rows, lanes) for r in range(3) for d in range(3)], 1
        )
        total = jnp.dot(window, bands[b], preferred_element_type=F32)
        return total.astype(BF16).reshape(span, rows, lanes)

    loads[0].wait()
    fill_bands(0)
    loads[1].wait()

    for b in range(BLOCKS):
        mean = whole_group(sums) / table_entries

        def squares(p, total):
            off = x_buf[piece(p)].astype(F32) - mean
            return total + by_eight(off * off)

        spread = whole_group(lax.fori_loop(0, PIECES, squares, no_sums)) / table_entries
        gains = gain[b : b + 1]
        scale = lax.rsqrt(spread + EPS) * jnp.concatenate([gains, gains], 1) * 0.5
        facts[b, 0:1] = mean
        facts[b, 1:2] = scale
        facts[b, 2:8] = jnp.full((6, lanes), clip[0], jnp.int32).astype(F32)
        down = soon if b == 0 else gives[1]
        if_so(gives[0], fact_copy(b, 0).start)
        if_so(down, fact_copy(b, 1).start)

        def own(p):
            activate(x_buf[piece(p)], p * span, mean, scale)

        own(EARLY - 1)
        own(EARLY)

        def make(p, carry):
            @pl.when(p + 1 < PIECES)
            def _():
                own(p + 1)

            spat[b, piece(p)] = convolve(b, p)
            for run, (_, last) in enumerate(RUNS[b]):

                @pl.when(p == last - 1)
                def _():
                    away = jnp.logical_and(sends_aside, aside(run, line))
                    if_so(away, copy_aside(b, run).start)
                    if_so(jnp.logical_and(gives[0], jnp.logical_not(away)), copy(b, 0, run).start)
                    if_so(down, copy(b, 1, run).start)

            return carry

        lax.fori_loop(EARLY, PIECES, make, 0)

        if b == 0:

            @pl.when(late)
            def _():
                pl.semaphore_wait(ready, 1)
                raw_copy(b, 1).start()
                fact_copy(b, 1).start()
                for run in range(len(RUNS[b])):
                    copy(b, 1, run).start()

        for slot in range(2):
            for what in (raw_copy, fact_copy):
                if_so(takes[slot], what(b, slot).wait_recv)
                if_so(gives[slot + 2], what(b, slot + 2).start)

        def own_early(p, carry):
            own(p)
            return carry

        lax.fori_loop(0, EARLY - 1, own_early, 0)

        def make_early(p, carry):
            spat[b, piece(p)] = convolve(b, p)
            return carry

        lax.fori_loop(0, EARLY, make_early, 0)

        def redo(slot):
            if slot > 1:
                raw_copy(b, slot).wait_recv()
                fact_copy(b, slot).wait_recv()
            mean = facts_in[b, slot, 0:1]
            scale = facts_in[b, slot, 1:2]

            def norm(p, carry):
                activate(raw[b, slot, piece(p)], p * span, mean, scale)
                return carry

            lax.fori_loop(0, EARLY, norm, 0)
            activate(raw[b, slot, EARLY * span :], EARLY * span, mean, scale)

            def conv(p, carry):
                came[b, slot, piece(p)] = convolve(b, p)
                return carry

            lax.fori_loop(0, EARLY, conv, 0)

        def redo_or_blank(slot):
            if_so(takes[slot], lambda: redo(slot))

            @pl.when(jnp.logical_not(takes[slot]))
            def _():
                came[b, slot] = jnp.zeros((tiles, rows, lanes), BF16)

        redo_or_blank(0)
        redo_or_blank(1)

        for run in range(len(RUNS[b])):
            for slot in range(2):
                if_so(takes[slot], copy(b, slot, run).wait_recv)
                if_so(gives[slot + 2], copy(b, slot + 2, run).start)

            @pl.when(jnp.logical_and(passes_on, aside(run, line - 1)))
            def _():
                copy_aside(b, run).wait_recv()
                pass_on(b, run).start()


        redo_or_blank(2)
        redo_or_blank(3)

        if b == 0:
            for slot in range(2):
                if_so(gives[slot], raw_copy(b, slot).wait_send)
            for later in range(1, BLOCKS):
                fill_bands(later)
            loads[2].wait()
            taps[...] = jnp.zeros_like(taps)
            for k in range(TAPS):
                slot = SLOT_OF_TAP[k]
                for c in range(BLOCKS):
                    if slot is None:
                        matrix = time[c, k]
                    else:
                        inside = here((k - TAPS // 2) * STEP).astype(F32)
                        same = (facts_in[0, slot, 2:3, :half] == facts[0, 2:3, :half]).astype(F32)
                        matrix = (time[c, k].astype(F32) * (same * inside)).astype(BF16)
                    for a in range(2):
                        at = k * lanes + a * half
                        taps[c, at : at + half, a * half : (a + 1) * half] = matrix

        def finish(p, sums):
            window = jnp.concatenate(
                [
                    (spat[b, piece(p)] if slot is None else came[b, slot, piece(p)]).reshape(span * rows, lanes)
                    for slot in SLOT_OF_TAP
                ],
                1,
            )
            update = jnp.dot(window, taps[b], preferred_element_type=F32).astype(BF16).astype(F32)
            value = (x_buf[piece(p)].astype(F32) + update.reshape(span, rows, lanes)).astype(BF16)
            if b + 1 < BLOCKS:
                x_buf[piece(p)] = value
                return sums + by_eight(value.astype(F32))
            for t in range(span):
                at = pl.multiple_of((p * span + t) * lanes, lanes)
                out[0, :, pl.ds(at, lanes)] = value[t]
            return sums

        def finish_arrived(p, sums):
            if b + 1 < BLOCKS:

                for slot in range(2):
                    if_so(jnp.logical_and(p == RAW_AT, gives[slot]), raw_copy(b + 1, slot).start)

            for run, (first, _) in enumerate(RUNS[b]):
                for slot in (2, 3):
                    if_so(jnp.logical_and(p == first, takes[slot]), copy(b, slot, run).wait_recv)
            return finish(p, sums)

        sums = lax.fori_loop(0, EARLY, finish, no_sums)
        sums = lax.fori_loop(EARLY, PIECES, finish_arrived, sums)

    for b in range(BLOCKS):
        for slot in range(4):
            if_so(gives[slot], fact_copy(b, slot).wait_send)
            if b > 0 or slot > 1:
                if_so(gives[slot], raw_copy(b, slot).wait_send)

            for run in range(len(RUNS[b])):
                if_so(gives[slot], copy(b, slot, run).wait_send)
        for run in range(len(RUNS[b])):
            if_so(jnp.logical_and(passes_on, aside(run, line - 1)), pass_on(b, run).wait_send)


def per_device(frames, clip_ids, norm_gain, space_kernel, time_kernel):
    _, rows, wide = frames.shape
    lanes = 2 * space_kernel.shape[-1]
    tiles = wide // lanes
    span = tiles // PIECES
    early = EARLY * span + 1
    hbm = pl.BlockSpec(memory_space=pl.ANY)
    frames, norm_gain, space_kernel, time_kernel = (
        pltpu.with_memory_space_constraint(x, pltpu.HBM) for x in (frames, norm_gain, space_kernel, time_kernel)
    )
    return pl.pallas_call(
        kernel,
        out_shape=jax.ShapeDtypeStruct(frames.shape, BF16),
        in_specs=[hbm, pl.BlockSpec(memory_space=pltpu.SMEM), hbm, hbm, hbm],
        out_specs=pl.BlockSpec(memory_space=pltpu.VMEM),
        scratch_shapes=[
            pltpu.VMEM((rows, wide), BF16),
            pltpu.VMEM(norm_gain.shape, F32),
            pltpu.VMEM(space_kernel.shape, BF16),
            pltpu.VMEM(time_kernel.shape, BF16),
            pltpu.VMEM((tiles, rows, lanes), BF16),
            pltpu.VMEM((span, rows + 16, lanes), F32),
            pltpu.VMEM((3, tiles + 2, rows, lanes), BF16),
            pltpu.VMEM((BLOCKS, tiles, rows, lanes), BF16),
            pltpu.VMEM((BLOCKS, 4, tiles, rows, lanes), BF16),
            pltpu.VMEM((BLOCKS, 4, early, rows, lanes), BF16),
            pltpu.VMEM((BLOCKS, 9 * lanes, lanes), BF16),
            pltpu.VMEM((BLOCKS, TAPS * lanes, lanes), BF16),
            pltpu.VMEM((BLOCKS, 8, lanes), F32),
            pltpu.VMEM((BLOCKS, 4, 8, lanes), F32),
            pltpu.VMEM((BLOCKS, tiles, rows, lanes), BF16),
            pltpu.SemaphoreType.DMA((3,)),
            pltpu.SemaphoreType.DMA((PIECES,)),
            pltpu.SemaphoreType.DMA((BLOCKS, 4, 4)),
            pltpu.SemaphoreType.DMA((BLOCKS, 4, 4)),
            pltpu.SemaphoreType.DMA((BLOCKS, 4)),
            pltpu.SemaphoreType.DMA((BLOCKS, 4)),
            pltpu.SemaphoreType.DMA((BLOCKS, 4)),
            pltpu.SemaphoreType.DMA((BLOCKS, 4)),
            pltpu.SemaphoreType.DMA((BLOCKS, 4)),
            pltpu.SemaphoreType.DMA((BLOCKS, 4)),
            pltpu.SemaphoreType.REGULAR,
        ],
        compiler_params=pltpu.CompilerParams(
            collective_id=0, has_side_effects=True, vmem_limit_bytes=48 << 20
        ),
        cost_estimate=pl.CostEstimate(flops=5_000_000_000, bytes_accessed=2_000_000, transcendentals=800_000),
    )(frames, clip_ids, norm_gain, space_kernel, time_kernel)


def solution(mesh):
    return jax.shard_map(
        per_device,
        mesh=mesh,
        in_specs=(P(("dp", "dev"), None, None), P(("dp", "dev")), P(), P(), P()),
        out_specs=P(("dp", "dev"), None, None),
        check_vma=False,
    )
```

```python
import jax
import jax.numpy as jnp
from jax import lax
from jax.experimental import pallas as pl
from jax.experimental.pallas import tpu as pltpu
from jax.sharding import PartitionSpec as P

BLOCKS = 2
TAPS = 5
STEP = 2
GROUP = 2
PIECES = 16
EARLY = 4
RAW_AT = 8
LINE = 32
RUNS = (((4, 8), (8, 12), (12, 16)), ((4, 8), (8, 12), (12, 15), (15, 16)))
EPS = 1e-06
MESH = pl.DeviceIdType.MESH
F32 = jnp.float32
BF16 = jnp.bfloat16
OFFSETS = (STEP, -STEP, 2 * STEP, -2 * STEP)
SLOT_OF_TAP = (2, 0, None, 1, 3)


def kernel(
    frames_hbm, clip, gain_hbm, space_hbm, time_hbm, out,
    frames, gain, space, time,
    x_buf, shifted, act, spat, came, raw, bands, taps, facts, facts_in, passing,
    load_sem, frame_sem, send_sem, recv_sem, raw_send, raw_recv, fact_send, fact_recv,
    pass_send, pass_recv, ready,
):
    count = lax.axis_size("dev")
    me = lax.axis_index("dev")
    tiles, rows, lanes = x_buf.shape
    half = lanes // 2
    span = tiles // PIECES
    wide = span * lanes
    early = raw.shape[2]
    table_entries = rows * tiles * 2 * GROUP

    def peer(offset):
        return {"dev": lax.rem(me + offset + count, count)}

    def here(offset):
        return jnp.logical_and(me + offset >= 0, me + offset < count)

    takes = [here(-offset) for offset in OFFSETS]
    gives = [here(STEP), here(-STEP)]
    gives += [jnp.logical_and(gives[0], takes[0]), jnp.logical_and(gives[1], takes[1])]

    def if_so(condition, action):
        pl.when(condition)(action)

    line = me // LINE
    at_start = lax.rem(me, LINE) < STEP
    at_end = lax.rem(me, LINE) >= LINE - STEP
    sends_aside = jnp.logical_and(at_end, me + LINE < count)
    passes_on = me >= count - STEP
    from_aside = jnp.logical_and(at_start, me >= LINE)

    core = lax.rem(me, STEP)

    def aside(run):
        return run >= 2

    seams = range(count // LINE - 1)

    barrier = pltpu.get_barrier_semaphore()

    def arrive(offset):
        pl.semaphore_signal(barrier, inc=1, device_id=peer(offset), device_id_type=MESH)

    if_so(here(-STEP), lambda: arrive(-STEP))
    for seam in seams:
        if_so(passes_on, lambda: arrive((seam + 1) * LINE - count))
    if_so(from_aside, lambda: arrive(count - STEP + core - me))

    def piece(p):
        return pl.ds(pl.multiple_of(p * span, span), span)

    def fetch(p):
        at = pl.ds(pl.multiple_of(p * wide, wide), wide)
        return pltpu.make_async_copy(frames_hbm.at[0, :, at], frames.at[:, at], frame_sem.at[p])

    def start_fetch(p, carry):
        fetch(p).start()
        return carry

    lax.fori_loop(0, PIECES, start_fetch, 0)
    loads = [
        pltpu.make_async_copy(source, target, load_sem.at[i])
        for i, (source, target) in enumerate(
            ((space_hbm, space), (gain_hbm, gain), (time_hbm, time))
        )
    ]
    for load in loads:
        load.start()

    shifted[...] = jnp.zeros_like(shifted)
    for r in range(3):
        act[r, 0] = jnp.zeros((rows, lanes), BF16)
        act[r, tiles + 1] = jnp.zeros((rows, lanes), BF16)
    bands[...] = jnp.zeros_like(bands)

    def copy(b, slot, run):
        first, last = RUNS[b][run]
        part = pl.ds(first * span, (last - first) * span)
        source = spat.at[b] if slot < 2 else came.at[b, slot - 2]
        return pltpu.make_async_remote_copy(
            src_ref=source.at[part], dst_ref=came.at[b, slot, part],
            send_sem=send_sem.at[b, slot, run], recv_sem=recv_sem.at[b, slot, run],
            device_id=peer(OFFSETS[slot % 2]), device_id_type=MESH,
        )

    def raw_copy(b, slot):
        source = x_buf.at[pl.ds(0, early)] if slot < 2 else raw.at[b, slot - 2]
        return pltpu.make_async_remote_copy(
            src_ref=source, dst_ref=raw.at[b, slot],
            send_sem=raw_send.at[b, slot], recv_sem=raw_recv.at[b, slot],
            device_id=peer(OFFSETS[slot % 2]), device_id_type=MESH,
        )

    def fact_copy(b, slot):
        source = facts.at[b] if slot < 2 else facts_in.at[b, slot - 2]
        return pltpu.make_async_remote_copy(
            src_ref=source, dst_ref=facts_in.at[b, slot],
            send_sem=fact_send.at[b, slot], recv_sem=fact_recv.at[b, slot],
            device_id=peer(OFFSETS[slot % 2]), device_id_type=MESH,
        )

    def copy_aside(b, seam, run):
        first, last = RUNS[b][run]
        part = pl.ds(first * span, (last - first) * span)
        return pltpu.make_async_remote_copy(
            src_ref=spat.at[b, part], dst_ref=passing.at[b, seam, part],
            send_sem=send_sem.at[b, 0, run], recv_sem=pass_recv.at[b, seam, run],
            device_id={"dev": count - STEP + core}, device_id_type=MESH,
        )

    def pass_on(b, seam, run):
        first, last = RUNS[b][run]
        part = pl.ds(first * span, (last - first) * span)
        return pltpu.make_async_remote_copy(
            src_ref=passing.at[b, seam, part], dst_ref=came.at[b, 0, part],
            send_sem=pass_send.at[b, seam, run], recv_sem=recv_sem.at[b, 0, run],
            device_id={"dev": (seam + 1) * LINE + core}, device_id_type=MESH,
        )

    lane = lax.broadcasted_iota(jnp.int32, (1, lanes), 1)

    def whole_group(sums):
        sums = jnp.sum(sums, axis=0, keepdims=True)
        both = sums + pltpu.roll(sums, half, 1)
        beside = jnp.where(lane % 2 == 0, pltpu.roll(both, lanes - 1, 1), pltpu.roll(both, 1, 1))
        return both + beside

    def by_eight(values):
        return jnp.sum(values.reshape(-1, 8, lanes), axis=0)

    no_sums = jnp.zeros((8, lanes), F32)

    def take(p, sums):
        fetch(p).wait()
        for t in range(span):
            at = pl.multiple_of((p * span + t) * lanes, lanes)
            tile = frames[:, pl.ds(at, lanes)]
            x_buf[p * span + t] = tile
            sums = sums + by_eight(tile.astype(F32))
        return sums

    sums = lax.fori_loop(0, EARLY + 1, take, no_sums)
    pl.semaphore_wait(barrier, sum(n * c.astype(jnp.int32) for n, c in ((1, gives[0]), (1, sends_aside), (len(seams), passes_on))))

    @pl.when(gives[0])
    def _():
        pl.semaphore_signal(ready, inc=1, device_id=peer(STEP), device_id_type=MESH)
        raw_copy(0, 0).start()

    soon = jnp.logical_and(gives[1], jnp.logical_not(at_start))
    late = jnp.logical_and(gives[1], at_start)

    @pl.when(soon)
    def _():
        pl.semaphore_wait(ready, 1)
        raw_copy(0, 1).start()
    sums = lax.fori_loop(EARLY + 1, PIECES, take, sums)

    def fill_bands(b):
        for r in range(3):
            for d in range(3):
                for a in range(2):
                    for c in range(2):
                        q = 2 * (d - 1) + a - c + 1
                        if 0 <= q <= 2:
                            at = (r * 3 + d) * lanes + a * half
                            bands[b, at : at + half, c * half : (c + 1) * half] = space[b, r, q]

    def activate(values, at, mean, scale):
        n = values.shape[0]
        u = (values.astype(F32) - mean) * scale
        value = u * (1.0 + jnp.tanh(u))
        shifted[:n, 8 : 8 + rows] = value
        where = pl.ds(at + 1, n)
        act[1, where] = value.astype(BF16)
        act[0, where] = shifted[:n, 7 : 7 + rows].astype(BF16)
        act[2, where] = shifted[:n, 9 : 9 + rows].astype(BF16)

    def convolve(b, p):
        window = jnp.concatenate(
            [act[r, pl.ds(p * span + d, span)].reshape(span * rows, lanes) for r in range(3) for d in range(3)], 1
        )
        total = jnp.dot(window, bands[b], preferred_element_type=F32)
        return total.astype(BF16).reshape(span, rows, lanes)

    loads[0].wait()
    fill_bands(0)
    loads[1].wait()

    for b in range(BLOCKS):
        mean = whole_group(sums) / table_entries

        def squares(p, total):
            off = x_buf[piece(p)].astype(F32) - mean
            return total + by_eight(off * off)

        spread = whole_group(lax.fori_loop(0, PIECES, squares, no_sums)) / table_entries
        gains = gain[b : b + 1]
        scale = lax.rsqrt(spread + EPS) * jnp.concatenate([gains, gains], 1) * 0.5
        facts[b, 0:1] = mean
        facts[b, 1:2] = scale
        facts[b, 2:8] = jnp.full((6, lanes), clip[0], jnp.int32).astype(F32)
        down = soon if b == 0 else gives[1]
        if_so(gives[0], fact_copy(b, 0).start)
        if_so(down, fact_copy(b, 1).start)

        def own(p):
            activate(x_buf[piece(p)], p * span, mean, scale)

        own(EARLY - 1)
        own(EARLY)

        def make(p, carry):
            @pl.when(p + 1 < PIECES)
            def _():
                own(p + 1)

            spat[b, piece(p)] = convolve(b, p)
            for run, (_, last) in enumerate(RUNS[b]):

                @pl.when(p == last - 1)
                def _():
                    if aside(run):
                        if_so(sends_aside, copy_aside(b, lax.rem(line, len(seams)), run).start)
                        if_so(jnp.logical_and(gives[0], jnp.logical_not(sends_aside)), copy(b, 0, run).start)
                    else:
                        if_so(gives[0], copy(b, 0, run).start)
                    if_so(down, copy(b, 1, run).start)

            return carry

        lax.fori_loop(EARLY, PIECES, make, 0)

        if b == 0:

            @pl.when(late)
            def _():
                pl.semaphore_wait(ready, 1)
                raw_copy(b, 1).start()
                fact_copy(b, 1).start()
                for run in range(len(RUNS[b])):
                    copy(b, 1, run).start()

        for slot in range(2):
            for what in (raw_copy, fact_copy):
                if_so(takes[slot], what(b, slot).wait_recv)
                if_so(gives[slot + 2], what(b, slot + 2).start)

        def own_early(p, carry):
            own(p)
            return carry

        lax.fori_loop(0, EARLY - 1, own_early, 0)

        def make_early(p, carry):
            spat[b, piece(p)] = convolve(b, p)
            return carry

        lax.fori_loop(0, EARLY, make_early, 0)

        def redo(slot):
            if slot > 1:
                raw_copy(b, slot).wait_recv()
                fact_copy(b, slot).wait_recv()
            mean = facts_in[b, slot, 0:1]
            scale = facts_in[b, slot, 1:2]

            def norm(p, carry):
                activate(raw[b, slot, piece(p)], p * span, mean, scale)
                return carry

            lax.fori_loop(0, EARLY, norm, 0)
            activate(raw[b, slot, EARLY * span :], EARLY * span, mean, scale)

            def conv(p, carry):
                came[b, slot, piece(p)] = convolve(b, p)
                return carry

            lax.fori_loop(0, EARLY, conv, 0)

        def redo_or_blank(slot):
            if_so(takes[slot], lambda: redo(slot))

            @pl.when(jnp.logical_not(takes[slot]))
            def _():
                came[b, slot] = jnp.zeros((tiles, rows, lanes), BF16)

        redo_or_blank(0)
        redo_or_blank(1)

        @pl.when(passes_on)
        def _():
            for run in filter(aside, range(len(RUNS[b]))):
                for seam in seams:
                    copy_aside(b, seam, run).wait_recv()
                    pass_on(b, seam, run).start()

        for run in range(len(RUNS[b])):
            for slot in range(2):
                if_so(takes[slot], copy(b, slot, run).wait_recv)
                if_so(gives[slot + 2], copy(b, slot + 2, run).start)


        redo_or_blank(2)
        redo_or_blank(3)

        if b == 0:
            for slot in range(2):
                if_so(gives[slot], raw_copy(b, slot).wait_send)
            for later in range(1, BLOCKS):
                fill_bands(later)
            loads[2].wait()
            taps[...] = jnp.zeros_like(taps)
            for k in range(TAPS):
                slot = SLOT_OF_TAP[k]
                for c in range(BLOCKS):
                    if slot is None:
                        matrix = time[c, k]
                    else:
                        inside = here((k - TAPS // 2) * STEP).astype(F32)
                        same = (facts_in[0, slot, 2:3, :half] == facts[0, 2:3, :half]).astype(F32)
                        matrix = (time[c, k].astype(F32) * (same * inside)).astype(BF16)
                    for a in range(2):
                        at = k * lanes + a * half
                        taps[c, at : at + half, a * half : (a + 1) * half] = matrix

        def finish(p, sums):
            window = jnp.concatenate(
                [
                    (spat[b, piece(p)] if slot is None else came[b, slot, piece(p)]).reshape(span * rows, lanes)
                    for slot in SLOT_OF_TAP
                ],
                1,
            )
            update = jnp.dot(window, taps[b], preferred_element_type=F32).astype(BF16).astype(F32)
            value = (x_buf[piece(p)].astype(F32) + update.reshape(span, rows, lanes)).astype(BF16)
            if b + 1 < BLOCKS:
                x_buf[piece(p)] = value
                return sums + by_eight(value.astype(F32))
            for t in range(span):
                at = pl.multiple_of((p * span + t) * lanes, lanes)
                out[0, :, pl.ds(at, lanes)] = value[t]
            return sums

        def finish_arrived(p, sums):
            if b + 1 < BLOCKS:

                for slot in range(2):
                    if_so(jnp.logical_and(p == RAW_AT, gives[slot]), raw_copy(b + 1, slot).start)

            for run, (first, _) in enumerate(RUNS[b]):
                for slot in (2, 3):
                    if_so(jnp.logical_and(p == first, takes[slot]), copy(b, slot, run).wait_recv)
            return finish(p, sums)

        sums = lax.fori_loop(0, EARLY, finish, no_sums)
        sums = lax.fori_loop(EARLY, PIECES, finish_arrived, sums)

    for b in range(BLOCKS):
        for slot in range(4):
            if_so(gives[slot], fact_copy(b, slot).wait_send)
            if b > 0 or slot > 1:
                if_so(gives[slot], raw_copy(b, slot).wait_send)

            for run in range(len(RUNS[b])):
                if_so(gives[slot], copy(b, slot, run).wait_send)
        for run in filter(aside, range(len(RUNS[b]))):
            for seam in seams:
                if_so(passes_on, pass_on(b, seam, run).wait_send)


def per_device(frames, clip_ids, norm_gain, space_kernel, time_kernel):
    _, rows, wide = frames.shape
    lanes = 2 * space_kernel.shape[-1]
    tiles = wide // lanes
    span = tiles // PIECES
    early = EARLY * span + 1
    hbm = pl.BlockSpec(memory_space=pl.ANY)
    frames, norm_gain, space_kernel, time_kernel = (
        pltpu.with_memory_space_constraint(x, pltpu.HBM) for x in (frames, norm_gain, space_kernel, time_kernel)
    )
    return pl.pallas_call(
        kernel,
        out_shape=jax.ShapeDtypeStruct(frames.shape, BF16),
        in_specs=[hbm, pl.BlockSpec(memory_space=pltpu.SMEM), hbm, hbm, hbm],
        out_specs=pl.BlockSpec(memory_space=pltpu.VMEM),
        scratch_shapes=[
            pltpu.VMEM((rows, wide), BF16),
            pltpu.VMEM(norm_gain.shape, F32),
            pltpu.VMEM(space_kernel.shape, BF16),
            pltpu.VMEM(time_kernel.shape, BF16),
            pltpu.VMEM((tiles, rows, lanes), BF16),
            pltpu.VMEM((span, rows + 16, lanes), F32),
            pltpu.VMEM((3, tiles + 2, rows, lanes), BF16),
            pltpu.VMEM((BLOCKS, tiles, rows, lanes), BF16),
            pltpu.VMEM((BLOCKS, 4, tiles, rows, lanes), BF16),
            pltpu.VMEM((BLOCKS, 4, early, rows, lanes), BF16),
            pltpu.VMEM((BLOCKS, 9 * lanes, lanes), BF16),
            pltpu.VMEM((BLOCKS, TAPS * lanes, lanes), BF16),
            pltpu.VMEM((BLOCKS, 8, lanes), F32),
            pltpu.VMEM((BLOCKS, 4, 8, lanes), F32),
            pltpu.VMEM((BLOCKS, 3, tiles, rows, lanes), BF16),
            pltpu.SemaphoreType.DMA((3,)),
            pltpu.SemaphoreType.DMA((PIECES,)),
            pltpu.SemaphoreType.DMA((BLOCKS, 4, 4)),
            pltpu.SemaphoreType.DMA((BLOCKS, 4, 4)),
            pltpu.SemaphoreType.DMA((BLOCKS, 4)),
            pltpu.SemaphoreType.DMA((BLOCKS, 4)),
            pltpu.SemaphoreType.DMA((BLOCKS, 4)),
            pltpu.SemaphoreType.DMA((BLOCKS, 4)),
            pltpu.SemaphoreType.DMA((BLOCKS, 3, 4)),
            pltpu.SemaphoreType.DMA((BLOCKS, 3, 4)),
            pltpu.SemaphoreType.REGULAR,
        ],
        compiler_params=pltpu.CompilerParams(
            collective_id=0, has_side_effects=True, vmem_limit_bytes=48 << 20
        ),
        cost_estimate=pl.CostEstimate(flops=5_000_000_000, bytes_accessed=2_000_000, transcendentals=800_000),
    )(frames, clip_ids, norm_gain, space_kernel, time_kernel)


def solution(mesh):
    return jax.shard_map(
        per_device,
        mesh=mesh,
        in_specs=(P(("dp", "dev"), None, None), P(("dp", "dev")), P(), P(), P()),
        out_specs=P(("dp", "dev"), None, None),
        check_vma=False,
    )
```

```python
import jax
import jax.numpy as jnp
from jax import lax
from jax.experimental import pallas as pl
from jax.experimental.pallas import tpu as pltpu
from jax.sharding import PartitionSpec as P

BLOCKS = 2
TAPS = 5
STEP = 2
GROUP = 2
PIECES = 16
EARLY = 4
RAW_AT = 8
RUNS = (((0, 4), (4, 8), (8, 12), (12, 16)), ((0, 4), (4, 8), (8, 12), (12, 15), (15, 16)))
EPS = 1e-06
MESH = pl.DeviceIdType.MESH
F32 = jnp.float32
BF16 = jnp.bfloat16
OFFSETS = (STEP, -STEP, 2 * STEP, -2 * STEP)
SLOT_OF_TAP = (2, 0, None, 1, 3)


def kernel(
    frames_hbm, clip, gain_hbm, space_hbm, time_hbm, out,
    frames, gain, space, time,
    x_buf, shifted, act, spat, came, raw, bands, taps, facts, facts_in,
    load_sem, frame_sem, send_sem, recv_sem, raw_send, raw_recv, fact_send, fact_recv,
):
    count = lax.axis_size("dev")
    me = lax.axis_index("dev")
    tiles, rows, lanes = x_buf.shape
    half = lanes // 2
    span = tiles // PIECES
    wide = span * lanes
    early = raw.shape[2]
    table_entries = rows * tiles * 2 * GROUP

    def peer(offset):
        return {"dev": lax.rem(me + offset + count, count)}

    def here(offset):
        return jnp.logical_and(me + offset >= 0, me + offset < count)

    takes = [here(-offset) for offset in OFFSETS]
    gives = [here(STEP), here(-STEP)]
    gives += [jnp.logical_and(gives[0], takes[0]), jnp.logical_and(gives[1], takes[1])]

    def if_so(condition, action):
        pl.when(condition)(action)

    barrier = pltpu.get_barrier_semaphore()
    for offset in OFFSETS:

        @pl.when(here(offset))
        def _():
            pl.semaphore_signal(barrier, inc=1, device_id=peer(offset), device_id_type=MESH)

    def piece(p):
        return pl.ds(pl.multiple_of(p * span, span), span)

    def fetch(p):
        at = pl.ds(pl.multiple_of(p * wide, wide), wide)
        return pltpu.make_async_copy(frames_hbm.at[0, :, at], frames.at[:, at], frame_sem.at[p])

    def start_fetch(p, carry):
        fetch(p).start()
        return carry

    lax.fori_loop(0, PIECES, start_fetch, 0)
    loads = [
        pltpu.make_async_copy(source, target, load_sem.at[i])
        for i, (source, target) in enumerate(
            ((space_hbm, space), (gain_hbm, gain), (time_hbm, time))
        )
    ]
    for load in loads:
        load.start()

    shifted[...] = jnp.zeros_like(shifted)
    for r in range(3):
        act[r, 0] = jnp.zeros((rows, lanes), BF16)
        act[r, tiles + 1] = jnp.zeros((rows, lanes), BF16)
    bands[...] = jnp.zeros_like(bands)

    def copy(b, slot, run):
        first, last = RUNS[b][run]
        part = pl.ds(first * span, (last - first) * span)
        source = spat.at[b] if slot < 2 else came.at[b, slot - 2]
        return pltpu.make_async_remote_copy(
            src_ref=source.at[part], dst_ref=came.at[b, slot, part],
            send_sem=send_sem.at[b, slot, run], recv_sem=recv_sem.at[b, slot, run],
            device_id=peer(OFFSETS[slot % 2]), device_id_type=MESH,
        )

    def raw_copy(b, slot):
        return pltpu.make_async_remote_copy(
            src_ref=x_buf.at[pl.ds(0, early)], dst_ref=raw.at[b, slot],
            send_sem=raw_send.at[b, slot], recv_sem=raw_recv.at[b, slot],
            device_id=peer(OFFSETS[slot % 2]), device_id_type=MESH,
        )

    def fact_copy(b, slot):
        return pltpu.make_async_remote_copy(
            src_ref=facts.at[b], dst_ref=facts_in.at[b, slot],
            send_sem=fact_send.at[b, slot], recv_sem=fact_recv.at[b, slot],
            device_id=peer(OFFSETS[slot]), device_id_type=MESH,
        )

    lane = lax.broadcasted_iota(jnp.int32, (1, lanes), 1)

    def whole_group(sums):
        sums = jnp.sum(sums, axis=0, keepdims=True)
        both = sums + pltpu.roll(sums, half, 1)
        beside = jnp.where(lane % 2 == 0, pltpu.roll(both, lanes - 1, 1), pltpu.roll(both, 1, 1))
        return both + beside

    def by_eight(values):
        return jnp.sum(values.reshape(-1, 8, lanes), axis=0)

    no_sums = jnp.zeros((8, lanes), F32)

    def take(p, sums):
        fetch(p).wait()
        for t in range(span):
            at = pl.multiple_of((p * span + t) * lanes, lanes)
            tile = frames[:, pl.ds(at, lanes)]
            x_buf[p * span + t] = tile
            sums = sums + by_eight(tile.astype(F32))
        return sums

    sums = lax.fori_loop(0, EARLY + 1, take, no_sums)
    pl.semaphore_wait(barrier, sum(here(offset).astype(jnp.int32) for offset in OFFSETS))
    for slot in range(2):
        if_so(gives[slot], raw_copy(0, slot).start)
    sums = lax.fori_loop(EARLY + 1, PIECES, take, sums)

    def fill_bands(b):
        for r in range(3):
            for d in range(3):
                for a in range(2):
                    for c in range(2):
                        q = 2 * (d - 1) + a - c + 1
                        if 0 <= q <= 2:
                            at = (r * 3 + d) * lanes + a * half
                            bands[b, at : at + half, c * half : (c + 1) * half] = space[b, r, q]

    def activate(values, at, mean, scale):
        n = values.shape[0]
        u = (values.astype(F32) - mean) * scale
        value = u * (1.0 + jnp.tanh(u))
        shifted[:n, 8 : 8 + rows] = value
        where = pl.ds(at + 1, n)
        act[1, where] = value.astype(BF16)
        act[0, where] = shifted[:n, 7 : 7 + rows].astype(BF16)
        act[2, where] = shifted[:n, 9 : 9 + rows].astype(BF16)

    def convolve(b, p):
        window = jnp.concatenate(
            [act[r, pl.ds(p * span + d, span)].reshape(span * rows, lanes) for r in range(3) for d in range(3)], 1
        )
        total = jnp.dot(window, bands[b], preferred_element_type=F32)
        return total.astype(BF16).reshape(span, rows, lanes)

    loads[0].wait()
    fill_bands(0)
    loads[1].wait()

    for b in range(BLOCKS):
        mean = whole_group(sums) / table_entries

        def squares(p, total):
            off = x_buf[piece(p)].astype(F32) - mean
            return total + by_eight(off * off)

        spread = whole_group(lax.fori_loop(0, PIECES, squares, no_sums)) / table_entries
        gains = gain[b : b + 1]
        scale = lax.rsqrt(spread + EPS) * jnp.concatenate([gains, gains], 1) * 0.5
        facts[b, 0:1] = mean
        facts[b, 1:2] = scale
        facts[b, 2:8] = jnp.full((6, lanes), clip[0], jnp.int32).astype(F32)
        for slot in range(4 if b == 0 else 2):
            if_so(here(OFFSETS[slot]), fact_copy(b, slot).start)

        def own(p):
            activate(x_buf[piece(p)], p * span, mean, scale)

        own(EARLY - 1)
        own(EARLY)

        def make(p, carry):
            @pl.when(p + 1 < PIECES)
            def _():
                own(p + 1)

            spat[b, piece(p)] = convolve(b, p)
            for run, (_, last) in enumerate(RUNS[b]):
                for slot in range(2 if run else 0):
                    if_so(jnp.logical_and(p == last - 1, gives[slot]), copy(b, slot, run).start)
            return carry

        lax.fori_loop(EARLY, PIECES, make, 0)

        for slot in range(2):
            if_so(takes[slot], raw_copy(b, slot).wait_recv)

        def own_early(p, carry):
            own(p)
            return carry

        lax.fori_loop(0, EARLY - 1, own_early, 0)

        def make_early(p, carry):
            spat[b, piece(p)] = convolve(b, p)
            return carry

        lax.fori_loop(0, EARLY, make_early, 0)

        def redo(slot):
            if slot > 1:
                if b == 0:
                    fact_copy(b, slot).wait_recv()
                copy(b, slot, 0).wait_recv()
                return
            fact_copy(b, slot).wait_recv()
            mean = facts_in[b, slot, 0:1]
            scale = facts_in[b, slot, 1:2]

            def norm(p, carry):
                activate(raw[b, slot, piece(p)], p * span, mean, scale)
                return carry

            lax.fori_loop(0, EARLY, norm, 0)
            activate(raw[b, slot, EARLY * span :], EARLY * span, mean, scale)

            def conv(p, carry):
                came[b, slot, piece(p)] = convolve(b, p)
                return carry

            lax.fori_loop(0, EARLY, conv, 0)

        def redo_or_blank(slot):
            if_so(takes[slot], lambda: redo(slot))

            @pl.when(jnp.logical_not(takes[slot]))
            def _():
                came[b, slot] = jnp.zeros((tiles, rows, lanes), BF16)

        redo_or_blank(0)
        redo_or_blank(1)

        for run in range(len(RUNS[b])):
            for slot in range(2):
                if run:
                    if_so(takes[slot], copy(b, slot, run).wait_recv)
                if_so(gives[slot + 2], copy(b, slot + 2, run).start)

        redo_or_blank(2)
        redo_or_blank(3)

        if b == 0:
            for slot in range(2):
                if_so(gives[slot], raw_copy(b, slot).wait_send)
            for later in range(1, BLOCKS):
                fill_bands(later)
            loads[2].wait()
            taps[...] = jnp.zeros_like(taps)
            for k in range(TAPS):
                slot = SLOT_OF_TAP[k]
                for c in range(BLOCKS):
                    if slot is None:
                        matrix = time[c, k]
                    else:
                        inside = here((k - TAPS // 2) * STEP).astype(F32)
                        same = (facts_in[0, slot, 2:3, :half] == facts[0, 2:3, :half]).astype(F32)
                        matrix = (time[c, k].astype(F32) * (same * inside)).astype(BF16)
                    for a in range(2):
                        at = k * lanes + a * half
                        taps[c, at : at + half, a * half : (a + 1) * half] = matrix

        def finish(p, sums):
            window = jnp.concatenate(
                [
                    (spat[b, piece(p)] if slot is None else came[b, slot, piece(p)]).reshape(span * rows, lanes)
                    for slot in SLOT_OF_TAP
                ],
                1,
            )
            update = jnp.dot(window, taps[b], preferred_element_type=F32).astype(BF16).astype(F32)
            value = (x_buf[piece(p)].astype(F32) + update.reshape(span, rows, lanes)).astype(BF16)
            if b + 1 < BLOCKS:
                x_buf[piece(p)] = value
                return sums + by_eight(value.astype(F32))
            for t in range(span):
                at = pl.multiple_of((p * span + t) * lanes, lanes)
                out[0, :, pl.ds(at, lanes)] = value[t]
            return sums

        def finish_arrived(p, sums):
            if b + 1 < BLOCKS:

                for slot in range(2):
                    if_so(jnp.logical_and(p == RAW_AT, gives[slot]), raw_copy(b + 1, slot).start)

            for run, (first, _) in list(enumerate(RUNS[b]))[1:]:
                for slot in (2, 3):
                    if_so(jnp.logical_and(p == first, takes[slot]), copy(b, slot, run).wait_recv)
            return finish(p, sums)

        sums = lax.fori_loop(0, EARLY, finish, no_sums)
        sums = lax.fori_loop(EARLY, PIECES, finish_arrived, sums)

    for b in range(BLOCKS):
        for slot in range(4):
            if b == 0 or slot < 2:
                if_so(here(OFFSETS[slot]), fact_copy(b, slot).wait_send)
            if b > 0 and slot < 2:
                if_so(gives[slot], raw_copy(b, slot).wait_send)
            for run in range(1 if slot < 2 else 0, len(RUNS[b])):
                if_so(gives[slot], copy(b, slot, run).wait_send)


def per_device(frames, clip_ids, norm_gain, space_kernel, time_kernel):
    _, rows, wide = frames.shape
    lanes = 2 * space_kernel.shape[-1]
    tiles = wide // lanes
    span = tiles // PIECES
    early = EARLY * span + 1
    hbm = pl.BlockSpec(memory_space=pl.ANY)
    frames, norm_gain, space_kernel, time_kernel = (
        pltpu.with_memory_space_constraint(x, pltpu.HBM) for x in (frames, norm_gain, space_kernel, time_kernel)
    )
    return pl.pallas_call(
        kernel,
        out_shape=jax.ShapeDtypeStruct(frames.shape, BF16),
        in_specs=[hbm, pl.BlockSpec(memory_space=pltpu.SMEM), hbm, hbm, hbm],
        out_specs=pl.BlockSpec(memory_space=pltpu.VMEM),
        scratch_shapes=[
            pltpu.VMEM((rows, wide), BF16),
            pltpu.VMEM(norm_gain.shape, F32),
            pltpu.VMEM(space_kernel.shape, BF16),
            pltpu.VMEM(time_kernel.shape, BF16),
            pltpu.VMEM((tiles, rows, lanes), BF16),
            pltpu.VMEM((span, rows + 16, lanes), F32),
            pltpu.VMEM((3, tiles + 2, rows, lanes), BF16),
            pltpu.VMEM((BLOCKS, tiles, rows, lanes), BF16),
            pltpu.VMEM((BLOCKS, 4, tiles, rows, lanes), BF16),
            pltpu.VMEM((BLOCKS, 2, early, rows, lanes), BF16),
            pltpu.VMEM((BLOCKS, 9 * lanes, lanes), BF16),
            pltpu.VMEM((BLOCKS, TAPS * lanes, lanes), BF16),
            pltpu.VMEM((BLOCKS, 8, lanes), F32),
            pltpu.VMEM((BLOCKS, 4, 8, lanes), F32),
            pltpu.SemaphoreType.DMA((3,)),
            pltpu.SemaphoreType.DMA((PIECES,)),
            pltpu.SemaphoreType.DMA((BLOCKS, 4, 5)),
            pltpu.SemaphoreType.DMA((BLOCKS, 4, 5)),
            pltpu.SemaphoreType.DMA((BLOCKS, 4)),
            pltpu.SemaphoreType.DMA((BLOCKS, 4)),
            pltpu.SemaphoreType.DMA((BLOCKS, 4)),
            pltpu.SemaphoreType.DMA((BLOCKS, 4)),
        ],
        compiler_params=pltpu.CompilerParams(
            collective_id=0, has_side_effects=True, vmem_limit_bytes=48 << 20
        ),
        cost_estimate=pl.CostEstimate(flops=5_000_000_000, bytes_accessed=2_000_000, transcendentals=800_000),
    )(frames, clip_ids, norm_gain, space_kernel, time_kernel)


def solution(mesh):
    return jax.shard_map(
        per_device,
        mesh=mesh,
        in_specs=(P(("dp", "dev"), None, None), P(("dp", "dev")), P(), P(), P()),
        out_specs=P(("dp", "dev"), None, None),
        check_vma=False,
    )
```

```python
import jax
import jax.numpy as jnp
from jax import lax
from jax.experimental import pallas as pl
from jax.experimental.pallas import tpu as pltpu
from jax.sharding import PartitionSpec as P

BLOCKS = 2
TAPS = 5
STEP = 2
GROUP = 2
PIECES = 16
EARLY = 4
RAW_AT = 8
RUNS = (((0, 4), (4, 9), (9, 16)), ((0, 4), (4, 8), (8, 12), (12, 15), (15, 16)))
EPS = 1e-06
MESH = pl.DeviceIdType.MESH
F32 = jnp.float32
BF16 = jnp.bfloat16
OFFSETS = (STEP, -STEP, 2 * STEP, -2 * STEP)
SLOT_OF_TAP = (2, 0, None, 1, 3)


def kernel(
    frames_hbm, clip, gain_hbm, space_hbm, time_hbm, out,
    frames, gain, space, time,
    x_buf, shifted, act, spat, came, raw, bands, taps, facts, facts_in,
    load_sem, frame_sem, send_sem, recv_sem, raw_send, raw_recv, fact_send, fact_recv,
):
    count = lax.axis_size("dev")
    me = lax.axis_index("dev")
    tiles, rows, lanes = x_buf.shape
    half = lanes // 2
    span = tiles // PIECES
    wide = span * lanes
    early = raw.shape[2]
    table_entries = rows * tiles * 2 * GROUP

    def peer(offset):
        return {"dev": lax.rem(me + offset + count, count)}

    def here(offset):
        return jnp.logical_and(me + offset >= 0, me + offset < count)

    takes = [here(-offset) for offset in OFFSETS]
    gives = [here(STEP), here(-STEP)]
    gives += [jnp.logical_and(gives[0], takes[0]), jnp.logical_and(gives[1], takes[1])]

    def if_so(condition, action):
        pl.when(condition)(action)

    barrier = pltpu.get_barrier_semaphore()
    for offset in OFFSETS:

        @pl.when(here(offset))
        def _():
            pl.semaphore_signal(barrier, inc=1, device_id=peer(offset), device_id_type=MESH)

    def piece(p):
        return pl.ds(pl.multiple_of(p * span, span), span)

    def fetch(p):
        at = pl.ds(pl.multiple_of(p * wide, wide), wide)
        return pltpu.make_async_copy(frames_hbm.at[0, :, at], frames.at[:, at], frame_sem.at[p])

    def start_fetch(p, carry):
        fetch(p).start()
        return carry

    lax.fori_loop(0, PIECES, start_fetch, 0)
    loads = [
        pltpu.make_async_copy(source, target, load_sem.at[i])
        for i, (source, target) in enumerate(
            ((space_hbm, space), (gain_hbm, gain), (time_hbm, time))
        )
    ]
    for load in loads:
        load.start()

    shifted[...] = jnp.zeros_like(shifted)
    for r in range(3):
        act[r, 0] = jnp.zeros((rows, lanes), BF16)
        act[r, tiles + 1] = jnp.zeros((rows, lanes), BF16)
    bands[...] = jnp.zeros_like(bands)

    def copy(b, slot, run):
        first, last = RUNS[b][run]
        part = pl.ds(first * span, (last - first) * span)
        source = spat.at[b] if slot < 2 else came.at[b, slot - 2]
        return pltpu.make_async_remote_copy(
            src_ref=source.at[part], dst_ref=came.at[b, slot, part],
            send_sem=send_sem.at[b, slot, run], recv_sem=recv_sem.at[b, slot, run],
            device_id=peer(OFFSETS[slot % 2]), device_id_type=MESH,
        )

    def raw_copy(b, slot):
        return pltpu.make_async_remote_copy(
            src_ref=x_buf.at[pl.ds(0, early)], dst_ref=raw.at[b, slot],
            send_sem=raw_send.at[b, slot], recv_sem=raw_recv.at[b, slot],
            device_id=peer(OFFSETS[slot % 2]), device_id_type=MESH,
        )

    def fact_copy(b, slot):
        return pltpu.make_async_remote_copy(
            src_ref=facts.at[b], dst_ref=facts_in.at[b, slot],
            send_sem=fact_send.at[b, slot], recv_sem=fact_recv.at[b, slot],
            device_id=peer(OFFSETS[slot]), device_id_type=MESH,
        )

    lane = lax.broadcasted_iota(jnp.int32, (1, lanes), 1)

    def whole_group(sums):
        sums = jnp.sum(sums, axis=0, keepdims=True)
        both = sums + pltpu.roll(sums, half, 1)
        beside = jnp.where(lane % 2 == 0, pltpu.roll(both, lanes - 1, 1), pltpu.roll(both, 1, 1))
        return both + beside

    def by_eight(values):
        return jnp.sum(values.reshape(-1, 8, lanes), axis=0)

    no_sums = jnp.zeros((8, lanes), F32)

    def take(p, sums):
        fetch(p).wait()
        for t in range(span):
            at = pl.multiple_of((p * span + t) * lanes, lanes)
            tile = frames[:, pl.ds(at, lanes)]
            x_buf[p * span + t] = tile
            sums = sums + by_eight(tile.astype(F32))
        return sums

    sums = lax.fori_loop(0, EARLY + 1, take, no_sums)
    pl.semaphore_wait(barrier, sum(here(offset).astype(jnp.int32) for offset in OFFSETS))
    for slot in range(2):
        if_so(gives[slot], raw_copy(0, slot).start)
    sums = lax.fori_loop(EARLY + 1, PIECES, take, sums)

    def fill_bands(b):
        for r in range(3):
            for d in range(3):
                for a in range(2):
                    for c in range(2):
                        q = 2 * (d - 1) + a - c + 1
                        if 0 <= q <= 2:
                            at = (r * 3 + d) * lanes + a * half
                            bands[b, at : at + half, c * half : (c + 1) * half] = space[b, r, q]

    def activate(values, at, mean, scale):
        n = values.shape[0]
        u = (values.astype(F32) - mean) * scale
        value = u * (1.0 + jnp.tanh(u))
        shifted[:n, 8 : 8 + rows] = value
        where = pl.ds(at + 1, n)
        act[1, where] = value.astype(BF16)
        act[0, where] = shifted[:n, 7 : 7 + rows].astype(BF16)
        act[2, where] = shifted[:n, 9 : 9 + rows].astype(BF16)

    def convolve(b, p):
        window = jnp.concatenate(
            [act[r, pl.ds(p * span + d, span)].reshape(span * rows, lanes) for r in range(3) for d in range(3)], 1
        )
        total = jnp.dot(window, bands[b], preferred_element_type=F32)
        return total.astype(BF16).reshape(span, rows, lanes)

    loads[0].wait()
    fill_bands(0)
    loads[1].wait()

    for b in range(BLOCKS):
        mean = whole_group(sums) / table_entries

        def squares(p, total):
            off = x_buf[piece(p)].astype(F32) - mean
            return total + by_eight(off * off)

        spread = whole_group(lax.fori_loop(0, PIECES, squares, no_sums)) / table_entries
        gains = gain[b : b + 1]
        scale = lax.rsqrt(spread + EPS) * jnp.concatenate([gains, gains], 1) * 0.5
        facts[b, 0:1] = mean
        facts[b, 1:2] = scale
        facts[b, 2:8] = jnp.full((6, lanes), clip[0], jnp.int32).astype(F32)
        for slot in range(4 if b == 0 else 2):
            if_so(here(OFFSETS[slot]), fact_copy(b, slot).start)

        def own(p):
            activate(x_buf[piece(p)], p * span, mean, scale)

        own(EARLY - 1)
        own(EARLY)

        def make(p, carry):
            @pl.when(p + 1 < PIECES)
            def _():
                own(p + 1)

            spat[b, piece(p)] = convolve(b, p)
            for run, (_, last) in enumerate(RUNS[b]):
                for slot in range(2 if run else 0):
                    if_so(jnp.logical_and(p == last - 1, gives[slot]), copy(b, slot, run).start)
            return carry

        lax.fori_loop(EARLY, PIECES, make, 0)

        for slot in range(2):
            if_so(takes[slot], raw_copy(b, slot).wait_recv)

        def own_early(p, carry):
            own(p)
            return carry

        lax.fori_loop(0, EARLY - 1, own_early, 0)

        def make_early(p, carry):
            spat[b, piece(p)] = convolve(b, p)
            return carry

        lax.fori_loop(0, EARLY, make_early, 0)

        def redo(slot):
            if slot > 1:
                if b == 0:
                    fact_copy(b, slot).wait_recv()
                copy(b, slot, 0).wait_recv()
                return
            fact_copy(b, slot).wait_recv()
            mean = facts_in[b, slot, 0:1]
            scale = facts_in[b, slot, 1:2]

            def norm(p, carry):
                activate(raw[b, slot, piece(p)], p * span, mean, scale)
                return carry

            lax.fori_loop(0, EARLY, norm, 0)
            activate(raw[b, slot, EARLY * span :], EARLY * span, mean, scale)

            def conv(p, carry):
                came[b, slot, piece(p)] = convolve(b, p)
                return carry

            lax.fori_loop(0, EARLY, conv, 0)

        def redo_or_blank(slot):
            if_so(takes[slot], lambda: redo(slot))

            @pl.when(jnp.logical_not(takes[slot]))
            def _():
                came[b, slot] = jnp.zeros((tiles, rows, lanes), BF16)

        redo_or_blank(0)
        redo_or_blank(1)

        for run in range(len(RUNS[b])):
            for slot in range(2):
                if run:
                    if_so(takes[slot], copy(b, slot, run).wait_recv)
                if_so(gives[slot + 2], copy(b, slot + 2, run).start)

        redo_or_blank(2)
        redo_or_blank(3)

        if b == 0:
            for slot in range(2):
                if_so(gives[slot], raw_copy(b, slot).wait_send)
            for later in range(1, BLOCKS):
                fill_bands(later)
            loads[2].wait()
            taps[...] = jnp.zeros_like(taps)
            for k in range(TAPS):
                slot = SLOT_OF_TAP[k]
                for c in range(BLOCKS):
                    if slot is None:
                        matrix = time[c, k]
                    else:
                        inside = here((k - TAPS // 2) * STEP).astype(F32)
                        same = (facts_in[0, slot, 2:3, :half] == facts[0, 2:3, :half]).astype(F32)
                        matrix = (time[c, k].astype(F32) * (same * inside)).astype(BF16)
                    for a in range(2):
                        at = k * lanes + a * half
                        taps[c, at : at + half, a * half : (a + 1) * half] = matrix

        def finish(p, sums):
            window = jnp.concatenate(
                [
                    (spat[b, piece(p)] if slot is None else came[b, slot, piece(p)]).reshape(span * rows, lanes)
                    for slot in SLOT_OF_TAP
                ],
                1,
            )
            update = jnp.dot(window, taps[b], preferred_element_type=F32).astype(BF16).astype(F32)
            value = (x_buf[piece(p)].astype(F32) + update.reshape(span, rows, lanes)).astype(BF16)
            if b + 1 < BLOCKS:
                x_buf[piece(p)] = value
                return sums + by_eight(value.astype(F32))
            for t in range(span):
                at = pl.multiple_of((p * span + t) * lanes, lanes)
                out[0, :, pl.ds(at, lanes)] = value[t]
            return sums

        def finish_arrived(p, sums):
            if b + 1 < BLOCKS:

                for slot in range(2):
                    if_so(jnp.logical_and(p == RAW_AT, gives[slot]), raw_copy(b + 1, slot).start)

            for run, (first, _) in list(enumerate(RUNS[b]))[1:]:
                for slot in (2, 3):
                    if_so(jnp.logical_and(p == first, takes[slot]), copy(b, slot, run).wait_recv)
            return finish(p, sums)

        sums = lax.fori_loop(0, EARLY, finish, no_sums)
        sums = lax.fori_loop(EARLY, PIECES, finish_arrived, sums)

    for b in range(BLOCKS):
        for slot in range(4):
            if b == 0 or slot < 2:
                if_so(here(OFFSETS[slot]), fact_copy(b, slot).wait_send)
            if b > 0 and slot < 2:
                if_so(gives[slot], raw_copy(b, slot).wait_send)
            for run in range(1 if slot < 2 else 0, len(RUNS[b])):
                if_so(gives[slot], copy(b, slot, run).wait_send)


def per_device(frames, clip_ids, norm_gain, space_kernel, time_kernel):
    _, rows, wide = frames.shape
    lanes = 2 * space_kernel.shape[-1]
    tiles = wide // lanes
    span = tiles // PIECES
    early = EARLY * span + 1
    hbm = pl.BlockSpec(memory_space=pl.ANY)
    frames, norm_gain, space_kernel, time_kernel = (
        pltpu.with_memory_space_constraint(x, pltpu.HBM) for x in (frames, norm_gain, space_kernel, time_kernel)
    )
    return pl.pallas_call(
        kernel,
        out_shape=jax.ShapeDtypeStruct(frames.shape, BF16),
        in_specs=[hbm, pl.BlockSpec(memory_space=pltpu.SMEM), hbm, hbm, hbm],
        out_specs=pl.BlockSpec(memory_space=pltpu.VMEM),
        scratch_shapes=[
            pltpu.VMEM((rows, wide), BF16),
            pltpu.VMEM(norm_gain.shape, F32),
            pltpu.VMEM(space_kernel.shape, BF16),
            pltpu.VMEM(time_kernel.shape, BF16),
            pltpu.VMEM((tiles, rows, lanes), BF16),
            pltpu.VMEM((span, rows + 16, lanes), F32),
            pltpu.VMEM((3, tiles + 2, rows, lanes), BF16),
            pltpu.VMEM((BLOCKS, tiles, rows, lanes), BF16),
            pltpu.VMEM((BLOCKS, 4, tiles, rows, lanes), BF16),
            pltpu.VMEM((BLOCKS, 2, early, rows, lanes), BF16),
            pltpu.VMEM((BLOCKS, 9 * lanes, lanes), BF16),
            pltpu.VMEM((BLOCKS, TAPS * lanes, lanes), BF16),
            pltpu.VMEM((BLOCKS, 8, lanes), F32),
            pltpu.VMEM((BLOCKS, 4, 8, lanes), F32),
            pltpu.SemaphoreType.DMA((3,)),
            pltpu.SemaphoreType.DMA((PIECES,)),
            pltpu.SemaphoreType.DMA((BLOCKS, 4, 5)),
            pltpu.SemaphoreType.DMA((BLOCKS, 4, 5)),
            pltpu.SemaphoreType.DMA((BLOCKS, 4)),
            pltpu.SemaphoreType.DMA((BLOCKS, 4)),
            pltpu.SemaphoreType.DMA((BLOCKS, 4)),
            pltpu.SemaphoreType.DMA((BLOCKS, 4)),
        ],
        compiler_params=pltpu.CompilerParams(
            collective_id=0, has_side_effects=True, vmem_limit_bytes=48 << 20
        ),
        cost_estimate=pl.CostEstimate(flops=5_000_000_000, bytes_accessed=2_000_000, transcendentals=800_000),
    )(frames, clip_ids, norm_gain, space_kernel, time_kernel)


def solution(mesh):
    return jax.shard_map(
        per_device,
        mesh=mesh,
        in_specs=(P(("dp", "dev"), None, None), P(("dp", "dev")), P(), P(), P()),
        out_specs=P(("dp", "dev"), None, None),
        check_vma=False,
    )
```
